512 devices in a mesh: dp: 32 (over x, z), fsdp: 16 (over y, core).
Axes of the slice: x: 4, y: 8, z: 8, core: 2. Of those that a mesh axis runs over, the one named last changes fastest.
Arguments:
- gradient: bfloat16 [32, 1024, 8192], P('dp', 'fsdp'), may hold values from -40 to 40
- error: bfloat16 [32, 1024, 8192], P('dp', 'fsdp'), may hold values from -6 to 6
- warm_start: bfloat16 [8192, 64], P('fsdp'), may hold values from -6 to 6
Outputs:
- update: bfloat16 [1024, 8192], P('fsdp')
- new_error: bfloat16 [32, 1024, 8192], P('dp', 'fsdp')
The draws below stay inside these ranges and needn't reach their ends.
All inputs are finite; a program needn't handle non-finite values.
Results may differ from the reference program's by a relative error of at most 0.03.
Values may be sent and summed in bfloat16 or wider, within the bound.
A program may use at most 64 MiB of HBM per device.

```python
import jax
import jax.numpy as jnp
from jax import lax

D = 8192
RANK = 64
ITERS = 2
ROWS_TOTAL = 1024
N_DP = 32


def draw_gradient(key, part):
    key = jax.random.fold_in(key, 11)
    key_rows, key_cols, key_noise = jax.random.split(key, 3)
    row_scale = jnp.exp(jax.random.uniform(key_rows, (1, ROWS_TOTAL, 1), jnp.float32, jnp.log(0.3), jnp.log(3.0)))
    col_scale = jnp.exp(jax.random.uniform(key_cols, (1, 1, D), jnp.float32, jnp.log(0.4), jnp.log(4.0)))
    values = jax.random.normal(key_noise, (N_DP, ROWS_TOTAL, D), jnp.float32) * row_scale * col_scale
    return jnp.clip(values, -40.0, 40.0).astype(jnp.bfloat16)


def shard_levels(key, extent, shards, low, high):
    def one(position, blocks):
        draws = jax.random.uniform(jax.random.fold_in(jax.random.fold_in(key, 6), position), (blocks,), jnp.float32, low / len(shards), high / len(shards))
        return jnp.repeat(jnp.exp(draws), extent[position] // blocks).reshape((-1,) + (1,) * (len(extent) - position - 1))

    loudness = one(*shards[0])
    for cut in shards[1:]:
        loudness = loudness * one(*cut)
    return loudness


def normal_values(rng, extent, deviation, limit, cuts=(), kind=jnp.bfloat16):
    factor_of = shard_levels(rng, extent, cuts, -0.22, 0.18) if cuts else 1.0
    array = jax.random.normal(rng, extent, jnp.float32) * deviation * factor_of
    return jnp.minimum(jnp.maximum(array, -limit), limit).astype(kind)


def setup_inputs(seed: int = 0) -> dict:
    streams_of = jax.random.split(jax.random.key(seed), 4)
    return {
        "gradient": draw_gradient(jax.random.fold_in(streams_of[3], 71), 0),
        "error": normal_values(streams_of[1], (N_DP, ROWS_TOTAL, D), 1.0, 6.0, ((0, 32), (1, 16))),
        "warm_start": normal_values(streams_of[2], (D, RANK), 1.0, 6.0, ((0, 16),)),
    }


def reference(gradient, error, warm_start):
    merged = (gradient.astype(jnp.float32) + error.astype(jnp.float32)).astype(jnp.bfloat16)
    flat = merged.reshape(N_DP * ROWS_TOTAL, D)
    q_b = warm_start
    basis_b = None
    for iteration in range(ITERS):
        p_factor = jnp.dot(flat.astype(jnp.float32), q_b.astype(jnp.float32), preferred_element_type=jnp.float32).reshape(N_DP, ROWS_TOTAL, RANK).sum(0)
        gram_matrix = jnp.dot(p_factor.T, p_factor, precision=lax.Precision.HIGHEST)
        cholesky_factor = jnp.linalg.cholesky(gram_matrix)
        basis = jax.scipy.linalg.solve_triangular(cholesky_factor, p_factor.T, lower=True).T
        basis_b = basis.astype(jnp.bfloat16)
        stacked = jnp.tile(basis_b, (N_DP, 1))
        q_full = jnp.dot(flat.T.astype(jnp.float32), stacked.astype(jnp.float32), preferred_element_type=jnp.float32)
        q_b = q_full.astype(jnp.bfloat16)
    mean_f32 = jnp.dot(basis_b.astype(jnp.float32), q_b.T.astype(jnp.float32), preferred_element_type=jnp.float32) / N_DP
    update = mean_f32.astype(jnp.bfloat16)
    new_error = (merged.astype(jnp.float32) - mean_f32[None]).astype(jnp.bfloat16)
    return (update, new_error)
```

```python
import functools

import jax
import jax.numpy as jnp
from jax import lax
from jax.experimental import pallas as pl
from jax.experimental.pallas import tpu as pltpu
from jax.sharding import PartitionSpec as P

MESH = pl.DeviceIdType.MESH
F32, BF16 = jnp.float32, jnp.bfloat16
NX, NY, NZ = 4, 8, 8
RANK = 64
HALF = RANK // 2


def dot(a, b, contract=((1,), (0,))):
    return lax.dot_general(a, b, (contract, ((), ())), precision=lax.Precision.HIGHEST, preferred_element_type=F32)


def by_distance(n):
    return sorted(range(1, n), key=lambda o: (-min(o, n - o), o))


def pack(a):
    return jnp.concatenate([a[:HALF], a[HALF:]], axis=1)


def unpack(a):
    return jnp.concatenate([a[:, :RANK], a[:, RANK:]], axis=0)


def inverse_factor(packed):
    lane = lax.broadcasted_iota(jnp.int32, (8, 2 * RANK), 1)
    sub = lax.broadcasted_iota(jnp.int32, (8, 2 * RANK), 0)
    rolled = pltpu.roll(packed, RANK, 1)
    rows = []
    for b in range(RANK // 8):
        source = packed if b < HALF // 8 else rolled
        r = (8 * b) % HALF
        rows.append(jnp.where(lane < RANK, source[r : r + 8], (lane - RANK == sub + 8 * b).astype(F32)))
    for k in range(RANK):
        b, r = divmod(k, 8)
        pivot_row = rows[b][r : r + 1, :]
        scaled = pivot_row * (1.0 / pivot_row[:, k : k + 1])
        for i in range(b, RANK // 8):
            column = rows[i][:, k : k + 1]
            new = rows[i] - column * scaled
            rows[i] = jnp.where(sub > r, new, rows[i]) if i == b else new
    out = []
    for b in range(RANK // 8):
        diag = jnp.sum(jnp.where(lane == sub + 8 * b, rows[b], 0.0), axis=1, keepdims=True)
        out.append(rows[b] * lax.rsqrt(diag))
    return jnp.concatenate(out, axis=0)[:, RANK:]


def kernel(
    g_ref, e_ref, w_ref, upd_ref, err_ref,
    gv, ev, merged, xland, zsend, zland, m, q0, px, pz, gsend, gcore, gy, usend, ucore, uy, ufull, qland, upd, err,
    in_sem, out_sem, q0_send, q0_recv, xs_send, xs_recv, zs_send, zs_recv,
    px_send, px_recv, pz_send, pz_recv, gc_send, gc_recv, gy_send, gy_recv, uc_send, uc_recv, uy_send, uy_recv,
    uf_send, uf_recv, qz_send, qz_recv, qx_send, qx_recv, qc_send, qc_recv,
):
    nd, rows, cb = merged.shape
    wide = NZ * cb
    d, f = lax.axis_index("dp"), lax.axis_index("fsdp")
    x, z, y, k = d // NZ, d % NZ, f // 2, f % 2

    def at_x(o):
        return {"dp": ((x + o) % NX) * NZ + z, "fsdp": f}

    def at_z(o):
        return {"dp": x * NZ + (z + o) % NZ, "fsdp": f}

    def at_y(o):
        return {"dp": d, "fsdp": ((y + o) % NY) * 2 + k}

    partner = {"dp": d, "fsdp": y * 2 + 1 - k}

    def send(src, dst, ssem, rsem, to):
        copy = pltpu.make_async_remote_copy(
            src_ref=src, dst_ref=dst, send_sem=ssem, recv_sem=rsem, device_id=to, device_id_type=MESH
        )
        copy.start()
        return copy

    sent = []

    loads = []
    for i in range(NX):
        cols = pl.ds(i * wide, wide)
        for j, (src, dst) in enumerate(((g_ref, gv), (e_ref, ev))):
            copy = pltpu.make_async_copy(src.at[0, :, cols], dst.at[:, cols], in_sem.at[j, i])
            copy.start()
            loads.append(copy)

    barrier = pltpu.get_barrier_semaphore()
    greeted = [at_x(o) for o in range(1, NX)] + [at_z(o) for o in range(1, NZ)]
    greeted += [{"dp": d, "fsdp": (f + o) % (2 * NY)} for o in range(1, 2 * NY)]
    for to in greeted:
        pl.semaphore_signal(barrier, inc=1, device_id=to, device_id_type=MESH)

    per = w_ref.shape[0] // cb
    source = d // per
    part = d % per

    @pl.when(f == source)
    def _():
        q0[...] = w_ref[pl.ds(pl.multiple_of(part * cb, cb), cb), :].astype(F32).T.astype(BF16)

    for copy in loads:
        copy.wait()

    def merge(i, _):
        cols = pl.ds(pl.multiple_of(i * cb, cb), cb)
        merged[i] = (gv[:, cols].astype(F32) + ev[:, cols].astype(F32)).astype(BF16)
        return 0

    lax.fori_loop(0, nd, merge, 0)
    pl.semaphore_wait(barrier, len(greeted))

    zorder = by_distance(NZ) + [0]
    xcopies = []
    for i, o in enumerate(zorder):
        w = (z + o) % NZ
        xcopies.append([
            send(merged.at[((x + xo) % NX) * NZ + w], xland.at[xo - 1, i], xs_send.at[xo - 1, i], xs_recv.at[xo - 1, i], at_x(xo))
            for xo in by_distance(NX)
        ])
        sent += xcopies[-1]

    others = 2 * NY - 1

    def q0_copy(o):
        return pltpu.make_async_remote_copy(
            src_ref=q0, dst_ref=q0, send_sem=q0_send.at[o], recv_sem=q0_recv,
            device_id={"dp": d, "fsdp": (f + o + 1) % (2 * NY)}, device_id_type=MESH,
        )

    @pl.when(f == source)
    def _():
        for o in range(others):
            q0_copy(o).start()

    zcopies = []
    for i, o in enumerate(zorder):
        for copy in xcopies[i]:
            copy.wait_recv()
        total = merged[x * NZ + (z + o) % NZ].astype(F32)
        for j in range(NX - 1):
            total = total + xland[j, i].astype(F32)
        if o:
            zsend[i] = total.astype(BF16)
            zcopies.append(send(zsend.at[i], zland.at[i], zs_send.at[i], zs_recv.at[i], at_z(o)))
    for i, copy in enumerate(zcopies):
        copy.wait_recv()
        total = total + zland[i].astype(F32)
    sent += zcopies
    m[...] = total

    @pl.when(f != source)
    def _():
        q0_copy(0).wait_recv()

    @pl.when(f == source)
    def _():
        for o in range(others):
            q0_copy(o).wait_send()

    def sum_dp(value, use, beside=None):
        px[use, x] = pack(value)
        copies = [
            send(px.at[use, x], px.at[use, x], px_send.at[use, o - 1], px_recv.at[use, o - 1], at_x(o)) for o in by_distance(NX)
        ]
        for copy in copies:
            copy.wait_recv()
        total = px[use, 0]
        for i in range(1, NX):
            total = total + px[use, i]
        sent.extend(copies)
        pz[use, z] = total
        copies = [
            send(pz.at[use, z], pz.at[use, z], pz_send.at[use, o - 1], pz_recv.at[use, o - 1], at_z(o)) for o in by_distance(NZ)
        ]
        extra = beside() if beside is not None else None
        for copy in copies:
            copy.wait_recv()
        total = pz[use, 0]
        for i in range(1, NZ):
            total = total + pz[use, i]
        sent.extend(copies)
        return unpack(total), extra

    def sum_y(buf, use, ssem, rsem):
        copies = [send(buf.at[use, y], buf.at[use, y], ssem.at[use, o - 1], rsem.at[use, o - 1], at_y(o)) for o in by_distance(NY)]
        sent.extend(copies)

        def finish():
            for copy in copies:
                copy.wait_recv()
            total = buf[use, 0]
            for i in range(1, NY):
                total = total + buf[use, i]
            return total

        return finish

    def over_rows(p_t, use):
        gsend[use] = pack(dot(p_t, p_t, ((1,), (1,))))
        gram_copy = send(gsend.at[use], gcore.at[use], gc_send.at[use], gc_recv.at[use], partner)
        u_t = dot(p_t, m[...])
        half = cb // 2
        usend[use, 0] = u_t[:, :half]
        usend[use, 1] = u_t[:, half:]
        u_copy = send(usend.at[use, 1 - k], ucore.at[use], uc_send.at[use], uc_recv.at[use], partner)
        sent.extend([gram_copy, u_copy])
        gram_copy.wait_recv()
        gy[use, y] = gsend[use] + gcore[use]
        gram = sum_y(gy, use, gy_send, gy_recv)
        u_copy.wait_recv()
        uy[use, y] = usend[use, k] + ucore[use]
        u_half = sum_y(uy, use, uy_send, uy_recv)
        return gram, u_half

    p_t, _ = sum_dp(dot(q0[...].astype(F32), m[...], ((1,), (1,))), 0)
    gram, u_half = over_rows(p_t, 0)
    gram = gram()
    lane = lax.broadcasted_iota(jnp.int32, (HALF, 2 * RANK), 1)
    sub = lax.broadcasted_iota(jnp.int32, (HALF, 2 * RANK), 0)
    on_diag = (lane == sub) | (lane == sub + HALF + RANK)
    trace = jnp.sum(jnp.sum(jnp.where(on_diag, gram, 0.0), axis=1, keepdims=True), axis=0, keepdims=True)
    scale = lax.rsqrt(trace)
    ufull[k] = u_half() * scale
    u_copy = send(ufull.at[k], ufull.at[k], uf_send, uf_recv, partner)
    u_copy.wait_recv()
    sent.append(u_copy)
    u_t = jnp.concatenate([ufull[0], ufull[1]], axis=1)

    p_t, inverse = sum_dp(dot(u_t, m[...], ((1,), (1,))), 1, lambda: inverse_factor(gram * scale * scale))
    p_t = dot(inverse, p_t)
    gram, u_half = over_rows(p_t, 1)
    inverse = inverse_factor(gram())
    basis_b = dot(inverse, p_t).T.astype(BF16)
    qland[k, d] = dot(inverse, u_half()).astype(BF16)

    def q_z(o):
        return send(qland.at[k, d], qland.at[k, d], qz_send.at[o - 1], qz_recv.at[o - 1], at_z(o))

    def q_x(o, block):
        return [
            send(qland.at[k, block], qland.at[k, block], qx_send.at[xo - 1, o], qx_recv.at[xo - 1, o], at_x(xo))
            for xo in by_distance(NX)
        ]

    def q_core(slot, block):
        sent.append(send(qland.at[k, block], qland.at[k, block], qc_send.at[slot], qc_recv.at[slot], partner))

    zcopies = {o: q_z(o) for o in by_distance(NZ)}
    sent += zcopies.values()
    near = [0] + by_distance(NZ)[::-1]
    xcopies = {}
    for o in near:
        if o:
            zcopies[o].wait_recv()
        block = x * NZ + (z - o) % NZ
        xcopies[o] = q_x(o, block)
        sent += xcopies[o]
        q_core(o, block)
    for o in near:
        for copy, xo in zip(xcopies[o], by_distance(NX)):
            copy.wait_recv()
            q_core(xo * NZ + o, ((x - xo) % NX) * NZ + (z - o) % NZ)

    outs = []
    for xo in range(NX):
        xs = (x - xo) % NX

        def finish(o, _):
            block = xs * NZ + (z - o) % NZ
            pltpu.make_async_remote_copy(
                src_ref=qland.at[k, block], dst_ref=qland.at[1 - k, block],
                send_sem=qc_send.at[xo * NZ + o], recv_sem=qc_recv.at[xo * NZ + o],
                device_id=partner, device_id_type=MESH,
            ).wait_recv()
            q_t = jnp.concatenate([qland[0, block], qland[1, block]], axis=1)
            mean = jnp.dot(basis_b, q_t, preferred_element_type=F32) * (1.0 / nd)
            cols = pl.ds(pl.multiple_of(block * cb, cb), cb)
            upd[:, cols] = mean.astype(BF16)
            err[:, cols] = (merged[block].astype(F32) - mean).astype(BF16)
            return 0

        lax.fori_loop(0, NZ, finish, 0)
        cols = pl.ds(pl.multiple_of(xs * wide, wide), wide)
        for j, (src, dst) in enumerate(((upd, upd_ref), (err, err_ref.at[0]))):
            copy = pltpu.make_async_copy(src.at[:, cols], dst.at[:, cols], out_sem.at[j, xo])
            copy.start()
            outs.append(copy)
    for copy in sent:
        copy.wait_send()
    for copy in outs:
        copy.wait()


def on_device(gradient, error, warm_start):
    nd = NX * NZ
    _, rows, width = gradient.shape
    cb = width // nd
    dma = pltpu.SemaphoreType.DMA
    anywhere = pl.BlockSpec(memory_space=pl.ANY)
    return pl.pallas_call(
        kernel,
        out_shape=(
            jax.ShapeDtypeStruct((rows, width), BF16),
            jax.ShapeDtypeStruct((1, rows, width), BF16),
        ),
        in_specs=[anywhere, anywhere, pl.BlockSpec(memory_space=pltpu.VMEM)],
        out_specs=(anywhere, anywhere),
        scratch_shapes=[
            pltpu.VMEM((rows, width), BF16),
            pltpu.VMEM((rows, width), BF16),
            pltpu.VMEM((nd, rows, cb), BF16),
            pltpu.VMEM((NX - 1, NZ, rows, cb), BF16),
            pltpu.VMEM((NZ - 1, rows, cb), BF16),
            pltpu.VMEM((NZ - 1, rows, cb), BF16),
            pltpu.VMEM((rows, cb), F32),
            pltpu.VMEM((RANK, cb), BF16),
            pltpu.VMEM((2, NX, HALF, 2 * RANK), F32),
            pltpu.VMEM((2, NZ, HALF, 2 * RANK), F32),
            pltpu.VMEM((2, HALF, 2 * RANK), F32),
            pltpu.VMEM((2, HALF, 2 * RANK), F32),
            pltpu.VMEM((2, NY, HALF, 2 * RANK), F32),
            pltpu.VMEM((2, 2, RANK, cb // 2), F32),
            pltpu.VMEM((2, RANK, cb // 2), F32),
            pltpu.VMEM((2, NY, RANK, cb // 2), F32),
            pltpu.VMEM((2, RANK, cb // 2), F32),
            pltpu.VMEM((2, nd, RANK, cb // 2), BF16),
            pltpu.VMEM((rows, width), BF16),
            pltpu.VMEM((rows, width), BF16),
            dma((2, NX)), dma((2, NX)), dma((2 * NY - 1,)), dma,
            dma((NX - 1, NZ)), dma((NX - 1, NZ)), dma((NZ - 1,)), dma((NZ - 1,)),
            dma((2, NX - 1)), dma((2, NX - 1)), dma((2, NZ - 1)), dma((2, NZ - 1)),
            dma((2,)), dma((2,)), dma((2, NY - 1)), dma((2, NY - 1)),
            dma((2,)), dma((2,)), dma((2, NY - 1)), dma((2, NY - 1)),
            dma, dma, dma((NZ - 1,)), dma((NZ - 1,)), dma((NX - 1, NZ)), dma((NX - 1, NZ)), dma((nd,)), dma((nd,)),
        ],
        compiler_params=pltpu.CompilerParams(collective_id=0, has_side_effects=True, vmem_limit_bytes=32 << 20),
        cost_estimate=pl.CostEstimate(flops=4 * rows * width * RANK, bytes_accessed=8 * rows * width, transcendentals=0),
    )(gradient, error, warm_start)


def solution(mesh):
    return jax.shard_map(
        on_device,
        mesh=mesh,
        in_specs=(P("dp", "fsdp", None), P("dp", "fsdp", None), P("fsdp", None)),
        out_specs=(P("fsdp", None), P("dp", "fsdp", None)),
        check_vma=False,
    )
```

```python
import functools

import jax
import jax.numpy as jnp
from jax import lax
from jax.experimental import pallas as pl
from jax.experimental.pallas import tpu as pltpu
from jax.sharding import PartitionSpec as P

MESH = pl.DeviceIdType.MESH
F32, BF16 = jnp.float32, jnp.bfloat16
NX, NY, NZ = 4, 8, 8
RANK = 64
HALF = RANK // 2
TAIL = 16
GROUPS = 4


def split(a):
    high = a.astype(BF16)
    rest = a - high.astype(F32)
    middle = rest.astype(BF16)
    return jnp.concatenate([high, middle, (rest - middle.astype(F32)).astype(BF16)], axis=0)


def exact(a, b, contract=((1,), (0,))):
    terms = lax.dot_general(a, b, (contract, ((), ())), preferred_element_type=F32)
    return terms[:RANK] + (terms[RANK : 2 * RANK] + terms[2 * RANK :])


def dot(a, b):
    return jnp.dot(a, b, precision=lax.Precision.HIGHEST, preferred_element_type=F32)


def by_distance(n):
    return sorted(range(1, n), key=lambda o: (-min(o, n - o), o))


def pack(a):
    return jnp.concatenate([a[:HALF], a[HALF:]], axis=1)


def unpack(a):
    return jnp.concatenate([a[:, :RANK], a[:, RANK:]], axis=0)


def inverse_factor(packed):
    lane = lax.broadcasted_iota(jnp.int32, (8, 2 * RANK), 1)
    sub = lax.broadcasted_iota(jnp.int32, (8, 2 * RANK), 0)
    rolled = pltpu.roll(packed, RANK, 1)
    full, n = (8, 2 * RANK), RANK // 8
    a = []
    for b in range(n):
        source = packed if b < n // 2 else rolled
        r = (8 * b) % HALF
        a.append(jnp.where(lane < RANK, source[r : r + 8], (lane - RANK == sub + 8 * b).astype(F32)))
    for b in range(n):
        row = [jnp.broadcast_to(a[b][j : j + 1, :], full) for j in range(8)]
        diag = {(i, j): jnp.broadcast_to(row[i][:, 8 * b + j : 8 * b + j + 1], full) for i in range(8) for j in range(i, 8)}
        column = {(j, v): jnp.broadcast_to(a[v][:, 8 * b + j : 8 * b + j + 1], full) for j in range(8) for v in range(b + 1, n)}
        scaled = []
        for j in range(8):
            inverse = 1.0 / diag[j, j]
            for i in range(j + 1, 8):
                factor = diag[j, i] * inverse
                for c in range(i, 8):
                    diag[i, c] = diag[i, c] - factor * diag[j, c]
                row[i] = row[i] - factor * row[j]
                for v in range(b + 1, n):
                    column[i, v] = column[i, v] - factor * column[j, v]
            scaled.append(row[j] * inverse)
        for v in range(b + 1, n):
            for j in range(8):
                a[v] = a[v] - column[j, v] * scaled[j]
        for j in range(1, 8):
            a[b] = jnp.where(sub == j, row[j], a[b])
    out = []
    for b in range(n):
        pivot = jnp.sum(jnp.where(lane == sub + 8 * b, a[b], 0.0), axis=1, keepdims=True)
        out.append(a[b] * lax.rsqrt(pivot))
    return jnp.concatenate(out, axis=0)[:, RANK:]


def kernel(
    g_ref, e_ref, w_ref, qland, merged, basis,
    gv, ev, tails, xland, zsend, zland, tland, tsum, town, tx, mc, q0, px, pz, pf,
    in_sem, w_sem, q0_send, q0_recv, x_send, x_recv, z_send, z_recv, t_send, t_recv, tx_send, tx_recv,
    my_send, my_recv, mk_send, mk_recv, px_send, px_recv, pz_send, pz_recv, py_send, py_recv, pk_send, pk_recv,
    qz_send, qz_recv, qx_send, qx_recv, qk_send, qk_recv,
):
    nd, rows, cb = merged.shape
    body = rows - TAIL
    half = cb // 2
    d, f = lax.axis_index("dp"), lax.axis_index("fsdp")
    x, z, y, k = d // NZ, d % NZ, f // 2, f % 2

    def at_x(o):
        return {"dp": ((x + o) % NX) * NZ + z, "fsdp": f}

    def at_z(o):
        return {"dp": x * NZ + (z + o) % NZ, "fsdp": f}

    def at_y(o):
        return {"dp": d, "fsdp": ((y + o) % NY) * 2 + k}

    partner = {"dp": d, "fsdp": f + 1 - 2 * k}

    def remote(src, dst, ssem, rsem, to):
        return pltpu.make_async_remote_copy(
            src_ref=src, dst_ref=dst, send_sem=ssem, recv_sem=rsem, device_id=to, device_id_type=MESH
        )

    def send(src, dst, ssem, rsem, to):
        remote(src, dst, ssem, rsem, to).start()

    def arrived(as_much, sem):
        remote(as_much, as_much, sem, sem, partner).wait_recv()

    def left(as_much, sem):
        remote(as_much, as_much, sem, sem, partner).wait_send()

    loads = [pltpu.make_async_copy(g_ref.at[0], gv, in_sem.at[0]), pltpu.make_async_copy(e_ref.at[0], ev, in_sem.at[1])]
    for copy in loads:
        copy.start()

    barrier = pltpu.get_barrier_semaphore()
    greeted = [at_z(o) for o in by_distance(NZ)] + [at_y(o) for o in by_distance(NY)] + [at_x(o) for o in by_distance(NX)]
    greeted.append(partner)
    for to in greeted:
        pl.semaphore_signal(barrier, inc=1, device_id=to, device_id_type=MESH)

    per = w_ref.shape[1] // cb
    source = d // per
    w_copy = pltpu.make_async_copy(w_ref.at[:, pl.ds(pl.multiple_of((d % per) * cb, cb), cb)], q0, w_sem)
    is_source = f == source
    is_relay = (k == source % 2) & (y != source // 2)

    @pl.when(is_source)
    def _():
        w_copy.start()

    for copy in loads:
        copy.wait()

    zorder = by_distance(NZ) + [0]
    for i, o in enumerate(zorder):
        w = (z + o) % NZ
        for t in range(NX):
            block = t * NZ + w
            cols = pl.ds(pl.multiple_of(block * cb, cb), cb)
            value = (gv[:, cols].astype(F32) + ev[:, cols].astype(F32)).astype(BF16)
            merged[block] = value
            tails[i, t * TAIL : (t + 1) * TAIL] = value[body:]
    pl.semaphore_wait(barrier, len(greeted))

    def mine(i, xo):
        return ((x + xo) % NX) * NZ + (z + zorder[i]) % NZ

    for i, o in enumerate(zorder):
        if o:
            send(tails.at[i], tland.at[i], t_send, t_recv, at_z(o))
        for j, xo in enumerate(by_distance(NX)):
            send(merged.at[mine(i, xo), pl.ds(0, body)], xland.at[i, j], x_send, x_recv.at[i], at_x(xo))

    @pl.when(is_source)
    def _():
        w_copy.wait()
        send(q0, q0, q0_send, q0_recv, partner)
        for o in by_distance(NY):
            send(q0, q0, q0_send, q0_recv, at_y(o))

    def finish_tails():
        arrived(tland, t_recv)
        total = tails[NZ - 1].astype(F32)
        for i in range(NZ - 1):
            total = total + tland[i].astype(F32)
        town[...] = total
        tsum[...] = total.astype(BF16)
        for j, xo in enumerate(by_distance(NX)):
            rows_of = pl.ds(pl.multiple_of(((x + xo) % NX) * TAIL, TAIL), TAIL)
            send(tsum.at[rows_of], tx.at[j], tx_send, tx_recv, at_x(xo))

    for i, o in enumerate(zorder):
        if i == 6:
            finish_tails()

            @pl.when(is_relay)
            def _():
                arrived(q0, q0_recv)
                send(q0, q0, q0_send, q0_recv, partner)

        arrived(xland.at[i], x_recv.at[i])
        total = merged[mine(i, 0)][:body].astype(F32)
        for j in range(NX - 1):
            total = total + xland[i, j].astype(F32)
        if o:
            zsend[i] = total.astype(BF16)
            send(zsend.at[i], zland.at[i], z_send, z_recv, at_z(o))
    arrived(tx, tx_recv)
    tail = town[pl.ds(pl.multiple_of(x * TAIL, TAIL), TAIL), :]
    for j in range(NX - 1):
        tail = tail + tx[j].astype(F32)
    arrived(zland, z_recv)
    for i in range(NZ - 1):
        total = total + zland[i].astype(F32)
    m = jnp.concatenate([total, tail], axis=0).astype(BF16)

    @pl.when(~(is_source | is_relay))
    def _():
        arrived(q0, q0_recv)

    mc[k, y] = m
    for o in by_distance(NY):
        send(mc.at[k, y], mc.at[k, y], my_send, my_recv, at_y(o))

    def sum_dp(value, use, beside=None):
        px[use, x] = pack(value)
        for o in by_distance(NX):
            send(px.at[use, x], px.at[use, x], px_send, px_recv.at[use], at_x(o))
        arrived(px.at[use, pl.ds(0, NX - 1)], px_recv.at[use])
        total = (px[use, 0] + px[use, 1]) + (px[use, 2] + px[use, 3])
        pz[use, z] = total
        for o in by_distance(NZ):
            send(pz.at[use, z], pz.at[use, z], pz_send, pz_recv.at[use], at_z(o))
        extra = beside() if beside is not None else None
        arrived(pz.at[use, pl.ds(0, NZ - 1)], pz_recv.at[use])
        total = pz[use, 0]
        for i in range(1, NZ):
            total = total + pz[use, i]
        return total, extra

    lane = lax.broadcasted_iota(jnp.int32, (HALF, 2 * RANK), 1)
    sub = lax.broadcasted_iota(jnp.int32, (HALF, 2 * RANK), 0)

    def over_rows(packed, use):
        pf[use, k, y] = packed
        for o in by_distance(NY):
            send(pf.at[use, k, y], pf.at[use, k, y], py_send, py_recv.at[use], at_y(o))
        if use == 0:
            arrived(mc.at[k, pl.ds(0, NY - 1)], my_recv)
            send(mc.at[k], mc.at[k], mk_send, mk_recv, partner)
        arrived(pf.at[use, k, pl.ds(0, NY - 1)], py_recv.at[use])
        send(pf.at[use, k], pf.at[use, k], pk_send, pk_recv.at[use], partner)
        if use == 0:
            arrived(mc.at[1 - k], mk_recv)
        arrived(pf.at[use, 1 - k], pk_recv.at[use])
        u_t, gram = 0.0, 0.0
        for c in range(2):
            for i in range(0, NY, 4):
                parts = []
                for j in range(i, i + 4, 2):
                    one, two = pf[use, c, j], pf[use, c, j + 1]
                    upper = jnp.where(lane < RANK, one, pltpu.roll(two, RANK, 1))
                    lower = jnp.where(lane < RANK, pltpu.roll(one, RANK, 1), two)
                    parts.append(jnp.concatenate([upper, lower], axis=0))
                p = split(jnp.concatenate(parts, axis=1))
                u_t = u_t + exact(p, mc[c, i : i + 4].reshape(4 * rows, cb))
                gram = gram + exact(p, p, ((1,), (1,)))
        gram = gram[:, :RANK] + (gram[:, RANK : 2 * RANK] + gram[:, 2 * RANK :])
        return u_t, pack(gram)

    p, _ = sum_dp(
        lax.dot_general(q0[...], m, (((1,), (1,)), ((), ())), preferred_element_type=F32), 0
    )
    u_t, gram = over_rows(p, 0)
    on_diag = (lane == sub) | (lane == sub + HALF + RANK)
    trace = jnp.sum(jnp.sum(jnp.where(on_diag, gram, 0.0), axis=1, keepdims=True), axis=0, keepdims=True)
    scale = lax.rsqrt(trace)

    p, inverse = sum_dp(
        exact(split(u_t * scale), mc[k, y], ((1,), (1,))), 1, lambda: inverse_factor(gram * scale * scale)
    )
    p_t = dot(inverse, unpack(p))
    u_t, gram = over_rows(pack(p_t), 1)
    inverse = inverse_factor(gram)
    q_t = dot(inverse, u_t).astype(BF16)
    qland[0, d] = q_t[:, :half]
    qland[1, d] = q_t[:, half:]

    for o in by_distance(NZ):
        send(qland.at[k, d], qland.at[k, d], qz_send, qz_recv.at[o - 1], at_z(o))
    basis[...] = dot(inverse, p_t).T.astype(BF16)
    near = [0] + by_distance(NZ)[::-1]
    for o in near:
        block = x * NZ + (z - o) % NZ
        if o:
            arrived(qland.at[k, block], qz_recv.at[o - 1])
        for xo in by_distance(NX):
            send(qland.at[k, block], qland.at[k, block], qx_send, qx_recv.at[o], at_x(xo))
        if o:
            send(qland.at[k, block], qland.at[k, block], qk_send, qk_recv, partner)
    for o in near:
        arrived(qland.at[k, pl.ds(0, NX - 1)], qx_recv.at[o])
        for xo in by_distance(NX):
            block = ((x - xo) % NX) * NZ + (z - o) % NZ
            send(qland.at[k, block], qland.at[k, block], qk_send, qk_recv, partner)
    arrived(qland.at[1 - k, pl.ds(0, nd - 1)], qk_recv)

    left(xland, x_send)
    left(tland, t_send)
    left(tx, tx_send)
    left(zland, z_send)
    left(mc.at[k, pl.ds(0, NY - 1)], my_send)
    left(mc.at[k], mk_send)
    left(px.at[:, pl.ds(0, NX - 1)], px_send)
    left(pz.at[:, pl.ds(0, NZ - 1)], pz_send)
    left(pf.at[:, k, pl.ds(0, NY - 1)], py_send)
    left(pf.at[:, k], pk_send)
    left(qland.at[k, pl.ds(0, NZ - 1)], qz_send)
    left(qland.at[k, pl.ds(0, (NX - 1) * NZ)], qx_send)
    left(qland.at[k, pl.ds(0, nd - 1)], qk_send)

    @pl.when(is_source)
    def _():
        left(mc.at[k], q0_send)

    @pl.when(is_relay)
    def _():
        left(q0, q0_send)


def decompress(q_ref, merged, basis, upd_ref, err_ref, upd, err, sem):
    nd, rows, cb = merged.shape
    per = nd // GROUPS
    wide = per * cb
    left = basis[...]
    copies = []
    for i in range(GROUPS):
        for j in range(per):
            block = i * per + j
            q_t = jnp.concatenate([q_ref[0, block], q_ref[1, block]], axis=1)
            mean = jnp.dot(left, q_t, preferred_element_type=F32) * (1.0 / nd)
            cols = pl.ds(block * cb, cb)
            upd[:, cols] = mean.astype(BF16)
            err[:, cols] = (merged[block].astype(F32) - mean).astype(BF16)
        cols = pl.ds(i * wide, wide)
        for j, (src, dst) in enumerate(((upd, upd_ref), (err, err_ref.at[0]))):
            copy = pltpu.make_async_copy(src.at[:, cols], dst.at[:, cols], sem.at[j, i])
            copy.start()
            copies.append(copy)
    for copy in copies:
        copy.wait()


def on_device(gradient, error, warm_start):
    nd = NX * NZ
    _, rows, width = gradient.shape
    cb = width // nd
    dma = pltpu.SemaphoreType.DMA
    hbm = pl.BlockSpec(memory_space=pltpu.HBM)
    vmem = pl.BlockSpec(memory_space=pltpu.VMEM)
    small = (HALF, 2 * RANK)
    q, merged, basis = pl.pallas_call(
        kernel,
        out_shape=(
            pltpu.VMEM((2, nd, RANK, cb // 2), BF16),
            pltpu.VMEM((nd, rows, cb), BF16),
            pltpu.VMEM((rows, RANK), BF16),
        ),
        in_specs=[hbm, hbm, hbm],
        out_specs=(vmem, vmem, vmem),
        scratch_shapes=[
            pltpu.VMEM((rows, width), BF16),
            pltpu.VMEM((rows, width), BF16),
            pltpu.VMEM((NZ, NX * TAIL, cb), BF16),
            pltpu.VMEM((NZ, NX - 1, rows - TAIL, cb), BF16),
            pltpu.VMEM((NZ - 1, rows - TAIL, cb), BF16),
            pltpu.VMEM((NZ - 1, rows - TAIL, cb), BF16),
            pltpu.VMEM((NZ - 1, NX * TAIL, cb), BF16),
            pltpu.VMEM((NX * TAIL, cb), BF16),
            pltpu.VMEM((NX * TAIL, cb), F32),
            pltpu.VMEM((NX - 1, TAIL, cb), BF16),
            pltpu.VMEM((2, NY, rows, cb), BF16),
            pltpu.VMEM((RANK, cb), BF16),
            pltpu.VMEM((2, NX) + small, F32),
            pltpu.VMEM((2, NZ) + small, F32),
            pltpu.VMEM((2, 2, NY) + small, F32),
            dma((2,)), dma, dma, dma, dma, dma((NZ,)), dma, dma, dma, dma, dma, dma,
            dma, dma, dma, dma, dma, dma((2,)), dma, dma((2,)), dma, dma((2,)), dma, dma((2,)),
            dma, dma((NZ - 1,)), dma, dma((NZ,)), dma, dma,
        ],
        compiler_params=pltpu.CompilerParams(collective_id=0, has_side_effects=True, vmem_limit_bytes=32 << 20),
        cost_estimate=pl.CostEstimate(flops=4 * rows * width * RANK, bytes_accessed=8 * rows * width, transcendentals=0),
    )(*(pltpu.with_memory_space_constraint(v, pltpu.HBM) for v in (gradient, error, warm_start.T)))
    q, merged, basis = (pltpu.with_memory_space_constraint(v, pltpu.VMEM) for v in (q, merged, basis))
    return pl.pallas_call(
        decompress,
        out_shape=(jax.ShapeDtypeStruct((rows, width), BF16), jax.ShapeDtypeStruct((1, rows, width), BF16)),
        in_specs=[vmem, vmem, vmem],
        out_specs=(hbm, hbm),
        scratch_shapes=[pltpu.VMEM((rows, width), BF16), pltpu.VMEM((rows, width), BF16), dma((2, GROUPS))],
        compiler_params=pltpu.CompilerParams(vmem_limit_bytes=16 << 20),
        cost_estimate=pl.CostEstimate(flops=2 * rows * width * RANK, bytes_accessed=8 * rows * width, transcendentals=0),
    )(q, merged, basis)


def solution(mesh):
    return jax.shard_map(
        on_device,
        mesh=mesh,
        in_specs=(P("dp", "fsdp", None), P("dp", "fsdp", None), P("fsdp", None)),
        out_specs=(P("fsdp", None), P("dp", "fsdp", None)),
        check_vma=False,
    )
```

```python
import functools

import jax
import jax.numpy as jnp
from jax import lax
from jax.experimental import pallas as pl
from jax.experimental.pallas import tpu as pltpu
from jax.sharding import PartitionSpec as P

MESH = pl.DeviceIdType.MESH
F32, BF16 = jnp.float32, jnp.bfloat16
NX, NY, NZ = 4, 8, 8
RANK = 64
HALF = RANK // 2
TAIL = 32
GROUPS = 4


def split(a):
    high = a.astype(BF16)
    rest = a - high.astype(F32)
    middle = rest.astype(BF16)
    return jnp.concatenate([high, middle, (rest - middle.astype(F32)).astype(BF16)], axis=0)


def exact(a, b, contract=((1,), (0,))):
    terms = lax.dot_general(a, b, (contract, ((), ())), preferred_element_type=F32)
    return terms[:RANK] + (terms[RANK : 2 * RANK] + terms[2 * RANK :])


def dot(a, b):
    return jnp.dot(a, b, precision=lax.Precision.HIGHEST, preferred_element_type=F32)


def by_distance(n):
    return sorted(range(1, n), key=lambda o: (-min(o, n - o), o))


def pack(a):
    return jnp.concatenate([a[:HALF], a[HALF:]], axis=1)


def unpack(a):
    return jnp.concatenate([a[:, :RANK], a[:, RANK:]], axis=0)


def inverse_factor(packed):
    lane = lax.broadcasted_iota(jnp.int32, (8, 2 * RANK), 1)
    sub = lax.broadcasted_iota(jnp.int32, (8, 2 * RANK), 0)
    rolled = pltpu.roll(packed, RANK, 1)
    full, n = (8, 2 * RANK), RANK // 8
    a = []
    for b in range(n):
        source = packed if b < n // 2 else rolled
        r = (8 * b) % HALF
        a.append(jnp.where(lane < RANK, source[r : r + 8], (lane - RANK == sub + 8 * b).astype(F32)))
    for b in range(n):
        row = [jnp.broadcast_to(a[b][j : j + 1, :], full) for j in range(8)]
        diag = {(i, j): jnp.broadcast_to(row[i][:, 8 * b + j : 8 * b + j + 1], full) for i in range(8) for j in range(i, 8)}
        column = {(j, v): jnp.broadcast_to(a[v][:, 8 * b + j : 8 * b + j + 1], full) for j in range(8) for v in range(b + 1, n)}
        scaled = []
        for j in range(8):
            inverse = 1.0 / diag[j, j]
            for i in range(j + 1, 8):
                factor = diag[j, i] * inverse
                for c in range(i, 8):
                    diag[i, c] = diag[i, c] - factor * diag[j, c]
                row[i] = row[i] - factor * row[j]
                for v in range(b + 1, n):
                    column[i, v] = column[i, v] - factor * column[j, v]
            scaled.append(row[j] * inverse)
        for v in range(b + 1, n):
            for j in range(8):
                a[v] = a[v] - column[j, v] * scaled[j]
        for j in range(1, 8):
            a[b] = jnp.where(sub == j, row[j], a[b])
    out = []
    for b in range(n):
        pivot = jnp.sum(jnp.where(lane == sub + 8 * b, a[b], 0.0), axis=1, keepdims=True)
        out.append(a[b] * lax.rsqrt(pivot))
    return jnp.concatenate(out, axis=0)[:, RANK:]


def kernel(
    g_ref, e_ref, w_ref, qland, merged, basis,
    gv, ev, xland, zsend, zland, tland, tsum, tx, mc, q0, px, pz, pf,
    in_sem, w_sem, q0_send, q0_recv, x_send, x_recv, z_send, z_recv, t_send, t_recv, tx_send, tx_recv,
    my_send, my_recv, mk_send, mk_recv, px_send, px_recv, pz_send, pz_recv, py_send, py_recv, pk_send, pk_recv,
    qz_send, qz_recv, qx_send, qx_recv, qu_send, qu_recv, qv_send, qv_recv, qw_recv, qk_send, qk_recv,
):
    nd, rows, cb = merged.shape
    body = rows - TAIL
    half = cb // 2
    d, f = lax.axis_index("dp"), lax.axis_index("fsdp")
    x, z, y, k = d // NZ, d % NZ, f // 2, f % 2

    def at_x(o):
        return {"dp": ((x + o) % NX) * NZ + z, "fsdp": f}

    def at_z(o):
        return {"dp": x * NZ + (z + o) % NZ, "fsdp": f}

    def at_y(o):
        return {"dp": d, "fsdp": ((y + o) % NY) * 2 + k}

    partner = {"dp": d, "fsdp": f + 1 - 2 * k}

    def remote(src, dst, ssem, rsem, to):
        return pltpu.make_async_remote_copy(
            src_ref=src, dst_ref=dst, send_sem=ssem, recv_sem=rsem, device_id=to, device_id_type=MESH
        )

    def send(src, dst, ssem, rsem, to):
        remote(src, dst, ssem, rsem, to).start()

    def arrived(as_much, sem):
        remote(as_much, as_much, sem, sem, partner).wait_recv()

    def left(as_much, sem):
        remote(as_much, as_much, sem, sem, partner).wait_send()

    loads = [pltpu.make_async_copy(g_ref.at[0], gv, in_sem.at[0]), pltpu.make_async_copy(e_ref.at[0], ev, in_sem.at[1])]
    for copy in loads:
        copy.start()

    barrier = pltpu.get_barrier_semaphore()
    greeted = [at_z(o) for o in by_distance(NZ)] + [at_y(o) for o in by_distance(NY)] + [at_x(o) for o in by_distance(NX)]
    greeted.append(partner)
    for to in greeted:
        pl.semaphore_signal(barrier, inc=1, device_id=to, device_id_type=MESH)

    per = w_ref.shape[1] // cb
    source = d // per
    w_copy = pltpu.make_async_copy(w_ref.at[:, pl.ds(pl.multiple_of((d % per) * cb, cb), cb)], q0, w_sem)
    is_source = f == source
    is_relay = (k == source % 2) & (y != source // 2)

    @pl.when(is_source)
    def _():
        w_copy.start()

    for copy in loads:
        copy.wait()

    zorder = by_distance(NZ) + [0]
    for i, o in enumerate(zorder):
        w = (z + o) % NZ
        for t in range(NX):
            block = t * NZ + w
            cols = pl.ds(pl.multiple_of(block * cb, cb), cb)
            merged[block] = (gv[:, cols].astype(F32) + ev[:, cols].astype(F32)).astype(BF16)
    pl.semaphore_wait(barrier, len(greeted))

    def mine(i, xo):
        return ((x + xo) % NX) * NZ + (z + zorder[i]) % NZ

    opposite = NX // 2
    for i, o in enumerate(zorder):
        if o:
            send(merged.at[mine(i, opposite), pl.ds(body, TAIL)], tland.at[i], t_send, t_recv, at_z(o))
        send(merged.at[mine(i, opposite), pl.ds(0, body)], xland.at[i, pl.ds(2 * rows, body)], x_send, x_recv.at[i], at_x(opposite))
        for j in range(2):
            send(merged.at[mine(i, 1 - 2 * j)], xland.at[i, pl.ds(j * rows, rows)], x_send, x_recv.at[i], at_x(1 - 2 * j))

    @pl.when(is_source)
    def _():
        w_copy.wait()
        send(q0, q0, q0_send, q0_recv, partner)
        for o in by_distance(NY):
            send(q0, q0, q0_send, q0_recv, at_y(o))

    def finish_tails():
        arrived(tland, t_recv)
        total = merged[mine(NZ - 1, opposite)][body:].astype(F32)
        for i in range(NZ - 1):
            total = total + tland[i].astype(F32)
        tsum[...] = total.astype(BF16)
        send(tsum, tx, tx_send, tx_recv, at_x(opposite))

    for i, o in enumerate(zorder):
        if i == 6:
            finish_tails()

            @pl.when(is_relay)
            def _():
                arrived(q0, q0_recv)
                send(q0, q0, q0_send, q0_recv, partner)

        arrived(xland.at[i], x_recv.at[i])
        landed = xland[i].astype(F32)
        total = merged[mine(i, 0)].astype(F32) + (landed[:rows] + landed[rows : 2 * rows])
        total = jnp.concatenate([total[:body] + landed[2 * rows :], total[body:]], axis=0)
        if o:
            zsend[i] = total.astype(BF16)
            send(zsend.at[i], zland.at[i], z_send, z_recv, at_z(o))
    arrived(zland, z_recv)
    for i in range(NZ - 1):
        total = total + zland[i].astype(F32)
    arrived(tx, tx_recv)
    m = jnp.concatenate([total[:body], total[body:] + tx[...].astype(F32)], axis=0).astype(BF16)

    @pl.when(~(is_source | is_relay))
    def _():
        arrived(q0, q0_recv)

    mc[k, y] = m
    for o in by_distance(NY):
        send(mc.at[k, y], mc.at[k, y], my_send, my_recv, at_y(o))

    def sum_dp(value, use, beside=None):
        px[use, x] = pack(value)
        for o in by_distance(NX):
            send(px.at[use, x], px.at[use, x], px_send, px_recv.at[use], at_x(o))
        arrived(px.at[use, pl.ds(0, NX - 1)], px_recv.at[use])
        total = (px[use, 0] + px[use, 1]) + (px[use, 2] + px[use, 3])
        pz[use, z] = total
        for o in by_distance(NZ):
            send(pz.at[use, z], pz.at[use, z], pz_send, pz_recv.at[use], at_z(o))
        extra = beside() if beside is not None else None
        arrived(pz.at[use, pl.ds(0, NZ - 1)], pz_recv.at[use])
        total = pz[use, 0]
        for i in range(1, NZ):
            total = total + pz[use, i]
        return total, extra

    lane = lax.broadcasted_iota(jnp.int32, (HALF, 2 * RANK), 1)

    def over_rows(packed, use):
        pf[use, k, y] = packed
        for o in by_distance(NY):
            send(pf.at[use, k, y], pf.at[use, k, y], py_send, py_recv.at[use], at_y(o))
        if use == 0:
            arrived(mc.at[k, pl.ds(0, NY - 1)], my_recv)
            send(mc.at[k], mc.at[k], mk_send, mk_recv, partner)
        arrived(pf.at[use, k, pl.ds(0, NY - 1)], py_recv.at[use])
        send(pf.at[use, k], pf.at[use, k], pk_send, pk_recv.at[use], partner)

        def factors(c):
            terms = []
            for i in range(0, NY, 4):
                parts = []
                for j in range(i, i + 4, 2):
                    one, two = pf[use, c, j], pf[use, c, j + 1]
                    upper = jnp.where(lane < RANK, one, pltpu.roll(two, RANK, 1))
                    lower = jnp.where(lane < RANK, pltpu.roll(one, RANK, 1), two)
                    parts.append(jnp.concatenate([upper, lower], axis=0))
                terms.append(split(jnp.concatenate(parts, axis=1)))
            return terms

        def right(c, terms):
            return sum(exact(p, mc[c, 4 * i : 4 * i + 4].reshape(4 * rows, cb)) for i, p in enumerate(terms))

        def square(terms):
            return sum(exact(p, p, ((1,), (1,))) for p in terms)

        def squares(c):
            total = pf[use, c, 0] * pf[use, c, 0]
            for i in range(1, NY):
                total = total + pf[use, c, i] * pf[use, c, i]
            return total

        def finish(gram):
            return pack(gram[:, :RANK] + (gram[:, RANK : 2 * RANK] + gram[:, 2 * RANK :]))

        terms = factors(k)
        u_t = right(k, terms)
        if use == 0:
            norm = squares(k)
            arrived(mc.at[1 - k], mk_recv)
        else:
            gram = square(terms)
        arrived(pf.at[use, 1 - k], pk_recv.at[use])
        terms = factors(1 - k)
        u_t = u_t + right(1 - k, terms)
        if use == 0:
            norm = norm + squares(1 - k)
            norm = jnp.sum(jnp.sum(norm, axis=1, keepdims=True), axis=0, keepdims=True)
            return u_t, norm, lambda: finish(square(factors(0)) + square(factors(1)))
        return u_t, finish(gram + square(terms))

    p, _ = sum_dp(
        lax.dot_general(q0[...], m, (((1,), (1,)), ((), ())), preferred_element_type=F32), 0
    )
    u_t, norm, gram = over_rows(p, 0)
    scale = lax.rsqrt(norm)

    p, inverse = sum_dp(
        exact(split(u_t * scale), mc[k, y], ((1,), (1,))), 1, lambda: inverse_factor(gram() * scale * scale)
    )
    p_t = dot(inverse, unpack(p))
    u_t, gram = over_rows(pack(p_t), 1)
    inverse = inverse_factor(gram)
    q_t = dot(inverse, u_t)
    qland[k, d] = jnp.where(k == 0, q_t[:, :half], q_t[:, half:]).astype(BF16)

    for o in by_distance(NZ):
        send(qland.at[k, d], qland.at[k, d], qz_send, qz_recv.at[o - 1], at_z(o))
    first, last = pl.ds(0, HALF), pl.ds(HALF, HALF)

    def to_x(block, at):
        send(qland.at[k, block, first], qland.at[k, block, first], qu_send, qu_recv, at_x(opposite))
        for j in range(2):
            send(qland.at[k, block], qland.at[k, block], qx_send, qx_recv.at[at], at_x(1 - 2 * j))

    send(qland.at[k, d, last], qland.at[k, d, last], qv_send, qv_recv, at_x(opposite))
    to_x(d, 0)
    send(qland.at[k, d], qland.at[k, d], qk_send, qk_recv, partner)
    basis[...] = dot(inverse, p_t).T.astype(BF16)
    facing = ((x + opposite) % NX) * NZ
    near = by_distance(NZ)[::-1]
    for i, o in enumerate(near):
        block = x * NZ + (z - o) % NZ
        arrived(qland.at[k, block], qz_recv.at[o - 1])
        to_x(block, o)
        send(qland.at[k, block], qland.at[k, block], qk_send, qk_recv, partner)
        if i == 1:
            arrived(qland.at[k, facing + z, last], qv_recv)
            for zo in by_distance(NZ):
                send(qland.at[k, facing + z, last], qland.at[k, facing + z, last], qv_send, qw_recv, at_z(zo))
    for o in [0] + near:
        arrived(qland.at[k, pl.ds(0, 2)], qx_recv.at[o])
        for j in range(2):
            block = ((x + 1 - 2 * j) % NX) * NZ + (z - o) % NZ
            send(qland.at[k, block], qland.at[k, block], qk_send, qk_recv, partner)
    arrived(qland.at[k, pl.ds(0, NZ - 1), last], qw_recv)
    arrived(qland.at[k, pl.ds(0, NZ), first], qu_recv)
    send(qland.at[k, pl.ds(facing, NZ)], qland.at[k, pl.ds(facing, NZ)], qk_send, qk_recv, partner)
    arrived(qland.at[1 - k], qk_recv)

    left(xland, x_send)
    left(tland, t_send)
    left(tx, tx_send)
    left(zland, z_send)
    left(mc.at[k, pl.ds(0, NY - 1)], my_send)
    left(mc.at[k], mk_send)
    left(px.at[:, pl.ds(0, NX - 1)], px_send)
    left(pz.at[:, pl.ds(0, NZ - 1)], pz_send)
    left(pf.at[:, k, pl.ds(0, NY - 1)], py_send)
    left(pf.at[:, k], pk_send)
    left(qland.at[k, pl.ds(0, NZ - 1)], qz_send)
    left(qland.at[k, pl.ds(0, 2 * NZ)], qx_send)
    left(qland.at[k, pl.ds(0, NZ), first], qu_send)
    left(qland.at[k, pl.ds(0, NZ), last], qv_send)
    left(qland.at[k], qk_send)

    @pl.when(is_source)
    def _():
        left(mc.at[k], q0_send)

    @pl.when(is_relay)
    def _():
        left(q0, q0_send)


def decompress(q_ref, merged, basis, upd_ref, err_ref, upd, err, sem):
    nd, rows, cb = merged.shape
    per = nd // GROUPS
    wide = per * cb
    left = basis[...]
    copies = []
    for i in range(GROUPS):
        for j in range(per):
            block = i * per + j
            q_t = jnp.concatenate([q_ref[0, block], q_ref[1, block]], axis=1)
            mean = jnp.dot(left, q_t, preferred_element_type=F32) * (1.0 / nd)
            cols = pl.ds(block * cb, cb)
            upd[:, cols] = mean.astype(BF16)
            err[:, cols] = (merged[block].astype(F32) - mean).astype(BF16)
        cols = pl.ds(i * wide, wide)
        for j, (src, dst) in enumerate(((upd, upd_ref), (err, err_ref.at[0]))):
            copy = pltpu.make_async_copy(src.at[:, cols], dst.at[:, cols], sem.at[j, i])
            copy.start()
            copies.append(copy)
    for copy in copies:
        copy.wait()


def on_device(gradient, error, warm_start):
    nd = NX * NZ
    _, rows, width = gradient.shape
    cb = width // nd
    dma = pltpu.SemaphoreType.DMA
    hbm = pl.BlockSpec(memory_space=pltpu.HBM)
    vmem = pl.BlockSpec(memory_space=pltpu.VMEM)
    small = (HALF, 2 * RANK)
    q, merged, basis = pl.pallas_call(
        kernel,
        out_shape=(
            pltpu.VMEM((2, nd, RANK, cb // 2), BF16),
            pltpu.VMEM((nd, rows, cb), BF16),
            pltpu.VMEM((rows, RANK), BF16),
        ),
        in_specs=[hbm, hbm, hbm],
        out_specs=(vmem, vmem, vmem),
        scratch_shapes=[
            pltpu.VMEM((rows, width), BF16),
            pltpu.VMEM((rows, width), BF16),
            pltpu.VMEM((NZ, 3 * rows - TAIL, cb), BF16),
            pltpu.VMEM((NZ - 1, rows, cb), BF16),
            pltpu.VMEM((NZ - 1, rows, cb), BF16),
            pltpu.VMEM((NZ - 1, TAIL, cb), BF16),
            pltpu.VMEM((TAIL, cb), BF16),
            pltpu.VMEM((TAIL, cb), BF16),
            pltpu.VMEM((2, NY, rows, cb), BF16),
            pltpu.VMEM((RANK, cb), BF16),
            pltpu.VMEM((2, NX) + small, F32),
            pltpu.VMEM((2, NZ) + small, F32),
            pltpu.VMEM((2, 2, NY) + small, F32),
            dma((2,)), dma, dma, dma, dma, dma((NZ,)), dma, dma, dma, dma, dma, dma,
            dma, dma, dma, dma, dma, dma((2,)), dma, dma((2,)), dma, dma((2,)), dma, dma((2,)),
            dma, dma((NZ - 1,)), dma, dma((NZ,)), dma, dma, dma, dma, dma, dma, dma,
        ],
        compiler_params=pltpu.CompilerParams(collective_id=0, has_side_effects=True, vmem_limit_bytes=32 << 20),
        cost_estimate=pl.CostEstimate(flops=4 * rows * width * RANK, bytes_accessed=8 * rows * width, transcendentals=0),
    )(*(pltpu.with_memory_space_constraint(v, pltpu.HBM) for v in (gradient, error, warm_start.T)))
    q, merged, basis = (pltpu.with_memory_space_constraint(v, pltpu.VMEM) for v in (q, merged, basis))
    return pl.pallas_call(
        decompress,
        out_shape=(jax.ShapeDtypeStruct((rows, width), BF16), jax.ShapeDtypeStruct((1, rows, width), BF16)),
        in_specs=[vmem, vmem, vmem],
        out_specs=(hbm, hbm),
        scratch_shapes=[pltpu.VMEM((rows, width), BF16), pltpu.VMEM((rows, width), BF16), dma((2, GROUPS))],
        compiler_params=pltpu.CompilerParams(vmem_limit_bytes=16 << 20),
        cost_estimate=pl.CostEstimate(flops=2 * rows * width * RANK, bytes_accessed=8 * rows * width, transcendentals=0),
    )(q, merged, basis)


def solution(mesh):
    return jax.shard_map(
        on_device,
        mesh=mesh,
        in_specs=(P("dp", "fsdp", None), P("dp", "fsdp", None), P("fsdp", None)),
        out_specs=(P("fsdp", None), P("dp", "fsdp", None)),
        check_vma=False,
    )
```

```python
import functools

import jax
import jax.numpy as jnp
from jax import lax
from jax.experimental import pallas as pl
from jax.experimental.pallas import tpu as pltpu
from jax.sharding import PartitionSpec as P

MESH = pl.DeviceIdType.MESH
F32, BF16 = jnp.float32, jnp.bfloat16
NX, NY, NZ = 4, 8, 8
RANK = 64
HALF = RANK // 2
TAIL = 32
GROUPS = 4


def split(a):
    high = a.astype(BF16)
    rest = a - high.astype(F32)
    middle = rest.astype(BF16)
    return jnp.concatenate([high, middle, (rest - middle.astype(F32)).astype(BF16)], axis=0)


def exact(a, b, contract=((1,), (0,))):
    terms = lax.dot_general(a, b, (contract, ((), ())), preferred_element_type=F32)
    return terms[:RANK] + (terms[RANK : 2 * RANK] + terms[2 * RANK :])


def dot(a, b):
    return jnp.dot(a, b, precision=lax.Precision.HIGHEST, preferred_element_type=F32)


def by_distance(n):
    return sorted(range(1, n), key=lambda o: (-min(o, n - o), o))


def pack(a):
    return jnp.concatenate([a[:HALF], a[HALF:]], axis=1)


def unpack(a):
    return jnp.concatenate([a[:, :RANK], a[:, RANK:]], axis=0)


def inverse_factor(packed):
    lane = lax.broadcasted_iota(jnp.int32, (8, 2 * RANK), 1)
    sub = lax.broadcasted_iota(jnp.int32, (8, 2 * RANK), 0)
    rolled = pltpu.roll(packed, RANK, 1)
    full, n = (8, 2 * RANK), RANK // 8
    a = []
    for b in range(n):
        source = packed if b < n // 2 else rolled
        r = (8 * b) % HALF
        a.append(jnp.where(lane < RANK, source[r : r + 8], (lane - RANK == sub + 8 * b).astype(F32)))
    for b in range(n):
        row = [jnp.broadcast_to(a[b][j : j + 1, :], full) for j in range(8)]
        diag = {(i, j): jnp.broadcast_to(row[i][:, 8 * b + j : 8 * b + j + 1], full) for i in range(8) for j in range(i, 8)}
        column = {(j, v): jnp.broadcast_to(a[v][:, 8 * b + j : 8 * b + j + 1], full) for j in range(8) for v in range(b + 1, n)}
        scaled = []
        for j in range(8):
            inverse = 1.0 / diag[j, j]
            for i in range(j + 1, 8):
                factor = diag[j, i] * inverse
                for c in range(i, 8):
                    diag[i, c] = diag[i, c] - factor * diag[j, c]
                row[i] = row[i] - factor * row[j]
                for v in range(b + 1, n):
                    column[i, v] = column[i, v] - factor * column[j, v]
            scaled.append(row[j] * inverse)
        for v in range(b + 1, n):
            for j in range(8):
                a[v] = a[v] - column[j, v] * scaled[j]
        for j in range(1, 8):
            a[b] = jnp.where(sub == j, row[j], a[b])
    out = []
    for b in range(n):
        pivot = jnp.sum(jnp.where(lane == sub + 8 * b, a[b], 0.0), axis=1, keepdims=True)
        out.append(a[b] * lax.rsqrt(pivot))
    return jnp.concatenate(out, axis=0)[:, RANK:]


def kernel(
    g_ref, e_ref, w_ref, qland, merged, basis,
    gv, ev, xland, zsend, zland, tland, tsum, tx, mc, q0, px, pz, pf, gx, ux, nx,
    in_sem, w_sem, q0_send, q0_recv, x_send, x_recv, z_send, z_recv, t_send, t_recv, tx_send, tx_recv,
    my_send, my_recv, px_send, px_recv, pz_send, pz_recv, py_send, py_recv, gx_send, gx_recv, ux_send, ux_recv,
    nx_send, nx_recv,
    qz_send, qz_recv, qx_send, qx_recv, qu_send, qu_recv, qv_send, qv_recv, qw_recv, qk_send, qk_recv,
):
    nd, rows, cb = merged.shape
    body = rows - TAIL
    half = cb // 2
    d, f = lax.axis_index("dp"), lax.axis_index("fsdp")
    x, z, y, k = d // NZ, d % NZ, f // 2, f % 2

    def at_x(o):
        return {"dp": ((x + o) % NX) * NZ + z, "fsdp": f}

    def at_z(o):
        return {"dp": x * NZ + (z + o) % NZ, "fsdp": f}

    def at_y(o):
        return {"dp": d, "fsdp": ((y + o) % NY) * 2 + k}

    partner = {"dp": d, "fsdp": f + 1 - 2 * k}

    def remote(src, dst, ssem, rsem, to):
        return pltpu.make_async_remote_copy(
            src_ref=src, dst_ref=dst, send_sem=ssem, recv_sem=rsem, device_id=to, device_id_type=MESH
        )

    def send(src, dst, ssem, rsem, to):
        remote(src, dst, ssem, rsem, to).start()

    def arrived(as_much, sem):
        remote(as_much, as_much, sem, sem, partner).wait_recv()

    def left(as_much, sem):
        remote(as_much, as_much, sem, sem, partner).wait_send()

    loads = [pltpu.make_async_copy(g_ref.at[0], gv, in_sem.at[0]), pltpu.make_async_copy(e_ref.at[0], ev, in_sem.at[1])]
    for copy in loads:
        copy.start()

    barrier = pltpu.get_barrier_semaphore()
    greeted = [at_z(o) for o in by_distance(NZ)] + [at_y(o) for o in by_distance(NY)] + [at_x(o) for o in by_distance(NX)]
    greeted.append(partner)
    for to in greeted:
        pl.semaphore_signal(barrier, inc=1, device_id=to, device_id_type=MESH)

    per = w_ref.shape[1] // cb
    source = d // per
    w_copy = pltpu.make_async_copy(w_ref.at[:, pl.ds(pl.multiple_of((d % per) * cb, cb), cb)], q0, w_sem)
    is_source = f == source
    is_relay = (k == source % 2) & (y != source // 2)

    @pl.when(is_source)
    def _():
        w_copy.start()

    for copy in loads:
        copy.wait()

    zorder = by_distance(NZ) + [0]
    for i, o in enumerate(zorder):
        w = (z + o) % NZ
        for t in range(NX):
            block = t * NZ + w
            cols = pl.ds(pl.multiple_of(block * cb, cb), cb)
            merged[block] = (gv[:, cols].astype(F32) + ev[:, cols].astype(F32)).astype(BF16)
    pl.semaphore_wait(barrier, len(greeted))

    def mine(i, xo):
        return ((x + xo) % NX) * NZ + (z + zorder[i]) % NZ

    opposite = NX // 2
    pairs = [2, 1, 3, 0]

    def first_of(i):
        return 2 * ((z // 2 + pairs[i]) % (NZ // 2))

    def two(i, xo):
        return pl.ds(((x + xo) % NX) * NZ + first_of(i), 2)

    for i in range(NZ // 2):
        to = at_x(opposite)
        send(merged.at[two(i, opposite), pl.ds(0, body)], xland.at[i, :, pl.ds(2 * rows, body)], x_send, x_recv.at[i], to)
        for j in range(2):
            xo = 1 - 2 * j
            send(merged.at[two(i, xo)], xland.at[i, :, pl.ds(j * rows, rows)], x_send, x_recv.at[i], at_x(xo))
        for h in (2 * i, 2 * i + 1):
            if h < NZ - 1:
                send(merged.at[mine(h, opposite), pl.ds(body, TAIL)], tland.at[h], t_send, t_recv, at_z(zorder[h]))

    @pl.when(is_source)
    def _():
        w_copy.wait()
        send(q0, q0, q0_send, q0_recv, partner)
        for o in by_distance(NY):
            send(q0, q0, q0_send, q0_recv, at_y(o))

    def finish_tails():
        arrived(tland, t_recv)
        total = merged[mine(NZ - 1, opposite)][body:].astype(F32)
        for i in range(NZ - 1):
            total = total + tland[i].astype(F32)
        tsum[...] = total.astype(BF16)
        send(tsum, tx, tx_send, tx_recv, at_x(opposite))

    def block_sum(i, b):
        landed = xland[i, b].astype(F32)
        total = merged[x * NZ + first_of(i) + b].astype(F32) + (landed[:rows] + landed[rows : 2 * rows])
        return jnp.concatenate([total[:body] + landed[2 * rows :], total[body:]], axis=0)

    for i in range(NZ // 2):
        if i == NZ // 2 - 1:
            finish_tails()

            @pl.when(is_relay)
            def _():
                arrived(q0, q0_recv)
                send(q0, q0, q0_send, q0_recv, partner)

        arrived(xland.at[i], x_recv.at[i])
        for b in range(2) if i < NZ // 2 - 1 else (1 - z % 2,):
            at = 2 * i if i == NZ // 2 - 1 else 2 * i + b
            zsend[at] = block_sum(i, b).astype(BF16)
            to = {"dp": x * NZ + first_of(i) + b, "fsdp": f}
            send(zsend.at[at], zland.at[z], z_send, z_recv, to)
    total = block_sum(NZ // 2 - 1, z % 2)
    arrived(zland.at[pl.ds(0, NZ - 1)], z_recv)
    for o in range(1, NZ):
        total = total + zland[(z + o) % NZ].astype(F32)
    arrived(tx, tx_recv)
    m = jnp.concatenate([total[:body], total[body:] + tx[...].astype(F32)], axis=0).astype(BF16)

    @pl.when(~(is_source | is_relay))
    def _():
        arrived(q0, q0_recv)

    mc[y] = m
    for o in by_distance(NY):
        send(mc.at[y], mc.at[y], my_send, my_recv, at_y(o))

    def sum_dp(value, use, beside=None):
        px[use, x] = pack(value)
        for o in by_distance(NX):
            send(px.at[use, x], px.at[use, x], px_send, px_recv.at[use], at_x(o))
        arrived(px.at[use, pl.ds(0, NX - 1)], px_recv.at[use])
        total = (px[use, 0] + px[use, 1]) + (px[use, 2] + px[use, 3])
        pz[use, z] = total
        for o in by_distance(NZ):
            send(pz.at[use, z], pz.at[use, z], pz_send, pz_recv.at[use], at_z(o))
        extra = beside() if beside is not None else None
        arrived(pz.at[use, pl.ds(0, NZ - 1)], pz_recv.at[use])
        total = pz[use, 0]
        for i in range(1, NZ):
            total = total + pz[use, i]
        return total, extra

    lane = lax.broadcasted_iota(jnp.int32, (HALF, 2 * RANK), 1)

    def over_rows(packed, use):
        pf[use, y] = packed
        for o in by_distance(NY):
            send(pf.at[use, y], pf.at[use, y], py_send, py_recv.at[use], at_y(o))
        if use == 0:
            arrived(mc.at[pl.ds(0, NY - 1)], my_recv)
        arrived(pf.at[use, pl.ds(0, NY - 1)], py_recv.at[use])
        if use == 0:
            norm = pf[use, 0] * pf[use, 0]
            for i in range(1, NY):
                norm = norm + pf[use, i] * pf[use, i]
            nx[k] = (norm[:8] + norm[8:16]) + (norm[16:24] + norm[24:])
            send(nx.at[k], nx.at[k], nx_send, nx_recv, partner)
        terms = []
        for i in range(0, NY, 4):
            parts = []
            for j in range(i, i + 4, 2):
                one, two = pf[use, j], pf[use, j + 1]
                upper = jnp.where(lane < RANK, one, pltpu.roll(two, RANK, 1))
                lower = jnp.where(lane < RANK, pltpu.roll(one, RANK, 1), two)
                parts.append(jnp.concatenate([upper, lower], axis=0))
            terms.append(split(jnp.concatenate(parts, axis=1)))

        def start_gram():
            gram = sum(exact(p, p, ((1,), (1,))) for p in terms)
            gx[use, k] = pack(gram[:, :RANK] + (gram[:, RANK : 2 * RANK] + gram[:, 2 * RANK :]))
            send(gx.at[use, k], gx.at[use, k], gx_send, gx_recv.at[use], partner)

        def start_right():
            ux[use, k] = sum(exact(p, mc[4 * i : 4 * i + 4].reshape(4 * rows, cb)) for i, p in enumerate(terms))
            send(ux.at[use, k], ux.at[use, k], ux_send, ux_recv.at[use], partner)

        for start in (start_right, start_gram) if use == 0 else (start_gram, start_right):
            start()

        def gram():
            arrived(gx.at[use, 1 - k], gx_recv.at[use])
            return gx[use, 0] + gx[use, 1]

        def right():
            arrived(ux.at[use, 1 - k], ux_recv.at[use])
            return ux[use, 0] + ux[use, 1]

        return gram, right

    p, _ = sum_dp(
        lax.dot_general(q0[...], m, (((1,), (1,)), ((), ())), preferred_element_type=F32), 0
    )
    gram, right = over_rows(p, 0)
    arrived(nx.at[1 - k], nx_recv)
    scale = lax.rsqrt(jnp.sum(jnp.sum(nx[0] + nx[1], axis=0, keepdims=True), axis=1, keepdims=True))
    u_t = right()

    p, inverse = sum_dp(
        exact(split(u_t * scale), mc[y], ((1,), (1,))), 1, lambda: inverse_factor(gram() * scale * scale)
    )
    p_t = dot(inverse, unpack(p))
    gram, right = over_rows(pack(p_t), 1)
    inverse = inverse_factor(gram())
    q_t = dot(inverse, right())
    qland[k, d] = jnp.where(k == 0, q_t[:, :half], q_t[:, half:]).astype(BF16)

    for o in by_distance(NZ)[::-1]:
        send(qland.at[k, d], qland.at[k, d], qz_send, qz_recv.at[o - 1], at_z(o))
    first, last = pl.ds(0, HALF), pl.ds(HALF, HALF)

    def to_x(block, at):
        send(qland.at[k, block, first], qland.at[k, block, first], qu_send, qu_recv, at_x(opposite))
        for j in range(2):
            send(qland.at[k, block], qland.at[k, block], qx_send, qx_recv.at[at], at_x(1 - 2 * j))

    send(qland.at[k, d, last], qland.at[k, d, last], qv_send, qv_recv, at_x(opposite))
    to_x(d, 0)
    basis[...] = dot(inverse, p_t).T.astype(BF16)
    facing = ((x + opposite) % NX) * NZ
    near = by_distance(NZ)[::-1]
    for i, o in enumerate(near):
        block = x * NZ + (z - o) % NZ
        arrived(qland.at[k, block], qz_recv.at[o - 1])
        to_x(block, o)
        if i == 1:
            arrived(qland.at[k, facing + z, last], qv_recv)
            for zo in by_distance(NZ):
                send(qland.at[k, facing + z, last], qland.at[k, facing + z, last], qv_send, qw_recv, at_z(zo))
    column = qland.at[k, pl.ds(x * NZ, NZ)]
    send(column, column, qk_send, qk_recv, partner)
    for o in [0] + near:
        arrived(qland.at[k, pl.ds(0, 2)], qx_recv.at[o])
        for j in range(2):
            block = ((x + 1 - 2 * j) % NX) * NZ + (z - o) % NZ
            send(qland.at[k, block], qland.at[k, block], qk_send, qk_recv, partner)
    arrived(qland.at[k, pl.ds(0, NZ - 1), last], qw_recv)
    arrived(qland.at[k, pl.ds(0, NZ), first], qu_recv)
    send(qland.at[k, pl.ds(facing, NZ)], qland.at[k, pl.ds(facing, NZ)], qk_send, qk_recv, partner)
    arrived(qland.at[1 - k], qk_recv)

    left(xland, x_send)
    left(tland, t_send)
    left(tx, tx_send)
    left(zsend, z_send)
    left(mc.at[pl.ds(0, NY - 1)], my_send)
    left(px.at[:, pl.ds(0, NX - 1)], px_send)
    left(pz.at[:, pl.ds(0, NZ - 1)], pz_send)
    left(pf.at[:, pl.ds(0, NY - 1)], py_send)
    left(gx.at[:, k], gx_send)
    left(ux.at[:, k], ux_send)
    left(nx.at[k], nx_send)
    left(qland.at[k, pl.ds(0, NZ - 1)], qz_send)
    left(qland.at[k, pl.ds(0, 2 * NZ)], qx_send)
    left(qland.at[k, pl.ds(0, NZ), first], qu_send)
    left(qland.at[k, pl.ds(0, NZ), last], qv_send)
    left(qland.at[k], qk_send)

    @pl.when(is_source)
    def _():
        left(mc, q0_send)

    @pl.when(is_relay)
    def _():
        left(q0, q0_send)


def decompress(q_ref, merged, basis, upd_ref, err_ref, upd, err, sem):
    nd, rows, cb = merged.shape
    per = nd // GROUPS
    wide = per * cb
    left = basis[...]
    copies = []
    for i in range(GROUPS):
        for j in range(per):
            block = i * per + j
            q_t = jnp.concatenate([q_ref[0, block], q_ref[1, block]], axis=1)
            mean = jnp.dot(left, q_t, preferred_element_type=F32) * (1.0 / nd)
            cols = pl.ds(block * cb, cb)
            upd[:, cols] = mean.astype(BF16)
            err[:, cols] = (merged[block].astype(F32) - mean).astype(BF16)
        cols = pl.ds(i * wide, wide)
        for j, (src, dst) in enumerate(((upd, upd_ref), (err, err_ref.at[0]))):
            copy = pltpu.make_async_copy(src.at[:, cols], dst.at[:, cols], sem.at[j, i])
            copy.start()
            copies.append(copy)
    for copy in copies:
        copy.wait()


def on_device(gradient, error, warm_start):
    nd = NX * NZ
    _, rows, width = gradient.shape
    cb = width // nd
    dma = pltpu.SemaphoreType.DMA
    hbm = pl.BlockSpec(memory_space=pltpu.HBM)
    vmem = pl.BlockSpec(memory_space=pltpu.VMEM)
    small = (HALF, 2 * RANK)
    q, merged, basis = pl.pallas_call(
        kernel,
        out_shape=(
            pltpu.VMEM((2, nd, RANK, cb // 2), BF16),
            pltpu.VMEM((nd, rows, cb), BF16),
            pltpu.VMEM((rows, RANK), BF16),
        ),
        in_specs=[hbm, hbm, hbm],
        out_specs=(vmem, vmem, vmem),
        scratch_shapes=[
            pltpu.VMEM((rows, width), BF16),
            pltpu.VMEM((rows, width), BF16),
            pltpu.VMEM((NZ // 2, 2, 3 * rows - TAIL, cb), BF16),
            pltpu.VMEM((NZ - 1, rows, cb), BF16),
            pltpu.VMEM((NZ, rows, cb), BF16),
            pltpu.VMEM((NZ - 1, TAIL, cb), BF16),
            pltpu.VMEM((TAIL, cb), BF16),
            pltpu.VMEM((TAIL, cb), BF16),
            pltpu.VMEM((NY, rows, cb), BF16),
            pltpu.VMEM((RANK, cb), BF16),
            pltpu.VMEM((2, NX) + small, F32),
            pltpu.VMEM((2, NZ) + small, F32),
            pltpu.VMEM((2, NY) + small, F32),
            pltpu.VMEM((2, 2) + small, F32),
            pltpu.VMEM((2, 2, RANK, cb), F32),
            pltpu.VMEM((2, 8, 128), F32),
            dma((2,)), dma, dma, dma, dma, dma((NZ,)), dma, dma, dma, dma, dma, dma,
            dma, dma, dma, dma((2,)), dma, dma((2,)), dma, dma((2,)), dma, dma((2,)), dma, dma((2,)), dma, dma,
            dma, dma((NZ - 1,)), dma, dma((NZ,)), dma, dma, dma, dma, dma, dma, dma,
        ],
        compiler_params=pltpu.CompilerParams(collective_id=0, has_side_effects=True, vmem_limit_bytes=32 << 20),
        cost_estimate=pl.CostEstimate(flops=4 * rows * width * RANK, bytes_accessed=8 * rows * width, transcendentals=0),
    )(*(pltpu.with_memory_space_constraint(v, pltpu.HBM) for v in (gradient, error, warm_start.T)))
    q, merged, basis = (pltpu.with_memory_space_constraint(v, pltpu.VMEM) for v in (q, merged, basis))
    return pl.pallas_call(
        decompress,
        out_shape=(jax.ShapeDtypeStruct((rows, width), BF16), jax.ShapeDtypeStruct((1, rows, width), BF16)),
        in_specs=[vmem, vmem, vmem],
        out_specs=(hbm, hbm),
        scratch_shapes=[pltpu.VMEM((rows, width), BF16), pltpu.VMEM((rows, width), BF16), dma((2, GROUPS))],
        compiler_params=pltpu.CompilerParams(vmem_limit_bytes=16 << 20),
        cost_estimate=pl.CostEstimate(flops=2 * rows * width * RANK, bytes_accessed=8 * rows * width, transcendentals=0),
    )(q, merged, basis)


def solution(mesh):
    return jax.shard_map(
        on_device,
        mesh=mesh,
        in_specs=(P("dp", "fsdp", None), P("dp", "fsdp", None), P("fsdp", None)),
        out_specs=(P("fsdp", None), P("dp", "fsdp", None)),
        check_vma=False,
    )
```

```python
import functools

import jax
import jax.numpy as jnp
from jax import lax
from jax.experimental import pallas as pl
from jax.experimental.pallas import tpu as pltpu
from jax.sharding import PartitionSpec as P

MESH = pl.DeviceIdType.MESH
F32, BF16 = jnp.float32, jnp.bfloat16
NX, NY, NZ = 4, 8, 8
RANK = 64
HALF = RANK // 2
TAIL = 48
GROUPS = 4


def split(a):
    high = a.astype(BF16)
    rest = a - high.astype(F32)
    middle = rest.astype(BF16)
    return jnp.concatenate([high, middle, (rest - middle.astype(F32)).astype(BF16)], axis=0)


def exact(a, b, contract=((1,), (0,))):
    terms = lax.dot_general(a, b, (contract, ((), ())), preferred_element_type=F32)
    return terms[:RANK] + (terms[RANK : 2 * RANK] + terms[2 * RANK :])


def dot(a, b):
    return jnp.dot(a, b, precision=lax.Precision.HIGHEST, preferred_element_type=F32)


def by_distance(n):
    return sorted(range(1, n), key=lambda o: (-min(o, n - o), o))


def pack(a):
    return jnp.concatenate([a[:HALF], a[HALF:]], axis=1)


def unpack(a):
    return jnp.concatenate([a[:, :RANK], a[:, RANK:]], axis=0)


def inverse_factor(packed):
    lane = lax.broadcasted_iota(jnp.int32, (8, 2 * RANK), 1)
    sub = lax.broadcasted_iota(jnp.int32, (8, 2 * RANK), 0)
    rolled = pltpu.roll(packed, RANK, 1)
    full, n = (8, 2 * RANK), RANK // 8
    a = []
    for b in range(n):
        source = packed if b < n // 2 else rolled
        r = (8 * b) % HALF
        a.append(jnp.where(lane < RANK, source[r : r + 8], (lane - RANK == sub + 8 * b).astype(F32)))
    for b in range(n):
        row = [jnp.broadcast_to(a[b][j : j + 1, :], full) for j in range(8)]
        diag = {(i, j): jnp.broadcast_to(row[i][:, 8 * b + j : 8 * b + j + 1], full) for i in range(8) for j in range(i, 8)}
        column = {(j, v): jnp.broadcast_to(a[v][:, 8 * b + j : 8 * b + j + 1], full) for j in range(8) for v in range(b + 1, n)}
        scaled = []
        for j in range(8):
            inverse = 1.0 / diag[j, j]
            for i in range(j + 1, 8):
                factor = diag[j, i] * inverse
                for c in range(i, 8):
                    diag[i, c] = diag[i, c] - factor * diag[j, c]
                row[i] = row[i] - factor * row[j]
                for v in range(b + 1, n):
                    column[i, v] = column[i, v] - factor * column[j, v]
            scaled.append(row[j] * inverse)
        for v in range(b + 1, n):
            for j in range(8):
                a[v] = a[v] - column[j, v] * scaled[j]
        for j in range(1, 8):
            a[b] = jnp.where(sub == j, row[j], a[b])
    out = []
    for b in range(n):
        pivot = jnp.sum(jnp.where(lane == sub + 8 * b, a[b], 0.0), axis=1, keepdims=True)
        out.append(a[b] * lax.rsqrt(pivot))
    return jnp.concatenate(out, axis=0)[:, RANK:]


def kernel(
    g_ref, e_ref, w_ref, qland, merged, basis,
    gv, ev, xland, zsend, zland, tland, tsum, tx, mc, q0, px, pz, pf, gx, ux, nx,
    in_sem, w_sem, q0_send, q0_recv, x_send, x_recv, z_send, z_recv, t_send, t_recv, tx_send, tx_recv,
    my_send, my_recv, px_send, px_recv, pz_send, pz_recv, py_send, py_recv, gx_send, gx_recv, ux_send, ux_recv,
    nx_send, nx_recv,
    qz_send, qz_recv, qx_send, qx_recv, qu_send, qu_recv, qv_send, qv_recv, qw_recv, qk_send, qk_recv,
):
    nd, rows, cb = merged.shape
    body = rows - TAIL
    half = cb // 2
    d, f = lax.axis_index("dp"), lax.axis_index("fsdp")
    x, z, y, k = d // NZ, d % NZ, f // 2, f % 2

    def at_x(o):
        return {"dp": ((x + o) % NX) * NZ + z, "fsdp": f}

    def at_z(o):
        return {"dp": x * NZ + (z + o) % NZ, "fsdp": f}

    def at_y(o):
        return {"dp": d, "fsdp": ((y + o) % NY) * 2 + k}

    partner = {"dp": d, "fsdp": f + 1 - 2 * k}

    def remote(src, dst, ssem, rsem, to):
        return pltpu.make_async_remote_copy(
            src_ref=src, dst_ref=dst, send_sem=ssem, recv_sem=rsem, device_id=to, device_id_type=MESH
        )

    def send(src, dst, ssem, rsem, to):
        remote(src, dst, ssem, rsem, to).start()

    def arrived(as_much, sem):
        remote(as_much, as_much, sem, sem, partner).wait_recv()

    def left(as_much, sem):
        remote(as_much, as_much, sem, sem, partner).wait_send()

    loads = [pltpu.make_async_copy(g_ref.at[0], gv, in_sem.at[0]), pltpu.make_async_copy(e_ref.at[0], ev, in_sem.at[1])]
    for copy in loads:
        copy.start()

    barrier = pltpu.get_barrier_semaphore()
    greeted = [at_z(o) for o in by_distance(NZ)] + [at_y(o) for o in by_distance(NY)] + [at_x(o) for o in by_distance(NX)]
    greeted.append(partner)
    for to in greeted:
        pl.semaphore_signal(barrier, inc=1, device_id=to, device_id_type=MESH)

    per = w_ref.shape[1] // cb
    source = d // per
    w_copy = pltpu.make_async_copy(w_ref.at[:, pl.ds(pl.multiple_of((d % per) * cb, cb), cb)], q0, w_sem)
    is_source = f == source
    is_relay = (k == source % 2) & (y != source // 2)

    @pl.when(is_source)
    def _():
        w_copy.start()

    for copy in loads:
        copy.wait()

    zorder = by_distance(NZ) + [0]
    for i, o in enumerate(zorder):
        w = (z + o) % NZ
        for t in range(NX):
            block = t * NZ + w
            cols = pl.ds(pl.multiple_of(block * cb, cb), cb)
            merged[block] = (gv[:, cols].astype(F32) + ev[:, cols].astype(F32)).astype(BF16)
    pl.semaphore_wait(barrier, len(greeted))

    def mine(i, xo):
        return ((x + xo) % NX) * NZ + (z + zorder[i]) % NZ

    opposite = NX // 2
    pairs = [2, 1, 3, 0]

    def first_of(i):
        return 2 * ((z // 2 + pairs[i]) % (NZ // 2))

    def two(i, xo):
        return pl.ds(((x + xo) % NX) * NZ + first_of(i), 2)

    for i in range(NZ // 2):
        to = at_x(opposite)
        send(merged.at[two(i, opposite), pl.ds(0, body)], xland.at[i, :, pl.ds(2 * rows, body)], x_send, x_recv.at[i], to)
        for j in range(2):
            xo = 1 - 2 * j
            send(merged.at[two(i, xo)], xland.at[i, :, pl.ds(j * rows, rows)], x_send, x_recv.at[i], at_x(xo))
        for h in (2 * i, 2 * i + 1):
            if h < NZ - 1:
                send(merged.at[mine(h, opposite), pl.ds(body, TAIL)], tland.at[h], t_send, t_recv, at_z(zorder[h]))

    @pl.when(is_source)
    def _():
        w_copy.wait()
        send(q0, q0, q0_send, q0_recv, partner)
        for o in by_distance(NY):
            send(q0, q0, q0_send, q0_recv, at_y(o))

    def finish_tails():
        arrived(tland, t_recv)
        total = merged[mine(NZ - 1, opposite)][body:].astype(F32)
        for i in range(NZ - 1):
            total = total + tland[i].astype(F32)
        tsum[...] = total.astype(BF16)
        send(tsum, tx, tx_send, tx_recv, at_x(opposite))

    def block_sum(i, b):
        landed = xland[i, b].astype(F32)
        total = merged[x * NZ + first_of(i) + b].astype(F32) + (landed[:rows] + landed[rows : 2 * rows])
        return jnp.concatenate([total[:body] + landed[2 * rows :], total[body:]], axis=0)

    for i in range(NZ // 2):
        if i == NZ // 2 - 1:
            @pl.when(is_relay)
            def _():
                arrived(q0, q0_recv)
                send(q0, q0, q0_send, q0_recv, partner)

        arrived(xland.at[i], x_recv.at[i])
        if i == NZ // 2 - 1:
            finish_tails()
        for b in range(2) if i < NZ // 2 - 1 else (1 - z % 2,):
            at = 2 * i if i == NZ // 2 - 1 else 2 * i + b
            zsend[at] = block_sum(i, b).astype(BF16)
            to = {"dp": x * NZ + first_of(i) + b, "fsdp": f}
            send(zsend.at[at], zland.at[z], z_send, z_recv, to)
    total = block_sum(NZ // 2 - 1, z % 2)
    arrived(zland.at[pl.ds(0, NZ - 1)], z_recv)
    for o in range(1, NZ):
        total = total + zland[(z + o) % NZ].astype(F32)
    arrived(tx, tx_recv)
    m = jnp.concatenate([total[:body], total[body:] + tx[...].astype(F32)], axis=0).astype(BF16)

    @pl.when(~(is_source | is_relay))
    def _():
        arrived(q0, q0_recv)

    mc[y] = m
    for o in by_distance(NY):
        send(mc.at[y], mc.at[y], my_send, my_recv, at_y(o))

    def sum_dp(value, use, beside=None):
        px[use, x] = pack(value)
        for o in by_distance(NX):
            send(px.at[use, x], px.at[use, x], px_send, px_recv.at[use], at_x(o))
        arrived(px.at[use, pl.ds(0, NX - 1)], px_recv.at[use])
        total = (px[use, 0] + px[use, 1]) + (px[use, 2] + px[use, 3])
        pz[use, z] = total
        for o in by_distance(NZ):
            send(pz.at[use, z], pz.at[use, z], pz_send, pz_recv.at[use], at_z(o))
        extra = beside() if beside is not None else None
        arrived(pz.at[use, pl.ds(0, NZ - 1)], pz_recv.at[use])
        total = pz[use, 0]
        for i in range(1, NZ):
            total = total + pz[use, i]
        return total, extra

    lane = lax.broadcasted_iota(jnp.int32, (HALF, 2 * RANK), 1)

    def over_rows(packed, use, factor=None):
        pf[use, y] = packed
        for o in by_distance(NY):
            send(pf.at[use, y], pf.at[use, y], py_send, py_recv.at[use], at_y(o))
        if use == 0:
            arrived(mc.at[pl.ds(0, NY - 1)], my_recv)
        arrived(pf.at[use, pl.ds(0, NY - 1)], py_recv.at[use])
        if use == 0:
            norm = pf[use, 0] * pf[use, 0]
            for i in range(1, NY):
                norm = norm + pf[use, i] * pf[use, i]
            nx[k] = (norm[:8] + norm[8:16]) + (norm[16:24] + norm[24:])
            send(nx.at[k], nx.at[k], nx_send, nx_recv, partner)
        terms = []
        for i in range(0, NY, 4):
            parts = []
            for j in range(i, i + 4, 2):
                one, two = pf[use, j], pf[use, j + 1]
                upper = jnp.where(lane < RANK, one, pltpu.roll(two, RANK, 1))
                lower = jnp.where(lane < RANK, pltpu.roll(one, RANK, 1), two)
                parts.append(jnp.concatenate([upper, lower], axis=0))
            p = jnp.concatenate(parts, axis=1)
            terms.append(split(p if factor is None else dot(factor, p)))

        def start_gram():
            gram = sum(exact(p, p, ((1,), (1,))) for p in terms)
            gx[use, k] = pack(gram[:, :RANK] + (gram[:, RANK : 2 * RANK] + gram[:, 2 * RANK :]))
            send(gx.at[use, k], gx.at[use, k], gx_send, gx_recv.at[use], partner)

        def start_right():
            ux[use, k] = sum(exact(p, mc[4 * i : 4 * i + 4].reshape(4 * rows, cb)) for i, p in enumerate(terms))
            send(ux.at[use, k], ux.at[use, k], ux_send, ux_recv.at[use], partner)

        for start in (start_right, start_gram) if use == 0 else (start_gram, start_right):
            start()

        def gram():
            arrived(gx.at[use, 1 - k], gx_recv.at[use])
            return gx[use, 0] + gx[use, 1]

        def right():
            arrived(ux.at[use, 1 - k], ux_recv.at[use])
            return ux[use, 0] + ux[use, 1]

        return gram, right

    p, _ = sum_dp(
        lax.dot_general(q0[...], m, (((1,), (1,)), ((), ())), preferred_element_type=F32), 0
    )
    gram, right = over_rows(p, 0)
    arrived(nx.at[1 - k], nx_recv)
    scale = lax.rsqrt(jnp.sum(jnp.sum(nx[0] + nx[1], axis=0, keepdims=True), axis=1, keepdims=True))
    u_t = right()

    p, inverse = sum_dp(
        exact(split(u_t * scale), mc[y], ((1,), (1,))), 1, lambda: inverse_factor(gram() * scale * scale)
    )
    gram, right = over_rows(p, 1, inverse)
    p_t = dot(inverse, unpack(p))
    inverse = inverse_factor(gram())
    q_t = dot(inverse, right())
    qland[k, d] = jnp.where(k == 0, q_t[:, :half], q_t[:, half:]).astype(BF16)

    for o in by_distance(NZ)[::-1]:
        send(qland.at[k, d], qland.at[k, d], qz_send, qz_recv.at[o - 1], at_z(o))
    first, last = pl.ds(0, HALF), pl.ds(HALF, HALF)

    def to_x(block, at):
        send(qland.at[k, block, first], qland.at[k, block, first], qu_send, qu_recv, at_x(opposite))
        for j in range(2):
            send(qland.at[k, block], qland.at[k, block], qx_send, qx_recv.at[at], at_x(1 - 2 * j))

    send(qland.at[k, d, last], qland.at[k, d, last], qv_send, qv_recv, at_x(opposite))
    to_x(d, 0)
    basis[...] = dot(inverse, p_t).T.astype(BF16)
    facing = ((x + opposite) % NX) * NZ
    near = by_distance(NZ)[::-1]
    for i, o in enumerate(near):
        block = x * NZ + (z - o) % NZ
        arrived(qland.at[k, block], qz_recv.at[o - 1])
        to_x(block, o)
        if i == 1:
            arrived(qland.at[k, facing + z, last], qv_recv)
            for zo in by_distance(NZ):
                send(qland.at[k, facing + z, last], qland.at[k, facing + z, last], qv_send, qw_recv, at_z(zo))
    column = qland.at[k, pl.ds(x * NZ, NZ)]
    send(column, column, qk_send, qk_recv, partner)
    for o in [0] + near:
        arrived(qland.at[k, pl.ds(0, 2)], qx_recv.at[o])
        for j in range(2):
            block = ((x + 1 - 2 * j) % NX) * NZ + (z - o) % NZ
            send(qland.at[k, block], qland.at[k, block], qk_send, qk_recv, partner)
    arrived(qland.at[k, pl.ds(0, NZ - 1), last], qw_recv)
    arrived(qland.at[k, pl.ds(0, NZ), first], qu_recv)
    send(qland.at[k, pl.ds(facing, NZ)], qland.at[k, pl.ds(facing, NZ)], qk_send, qk_recv, partner)
    arrived(qland.at[1 - k], qk_recv)

    left(xland, x_send)
    left(tland, t_send)
    left(tx, tx_send)
    left(zsend, z_send)
    left(mc.at[pl.ds(0, NY - 1)], my_send)
    left(px.at[:, pl.ds(0, NX - 1)], px_send)
    left(pz.at[:, pl.ds(0, NZ - 1)], pz_send)
    left(pf.at[:, pl.ds(0, NY - 1)], py_send)
    left(gx.at[:, k], gx_send)
    left(ux.at[:, k], ux_send)
    left(nx.at[k], nx_send)
    left(qland.at[k, pl.ds(0, NZ - 1)], qz_send)
    left(qland.at[k, pl.ds(0, 2 * NZ)], qx_send)
    left(qland.at[k, pl.ds(0, NZ), first], qu_send)
    left(qland.at[k, pl.ds(0, NZ), last], qv_send)
    left(qland.at[k], qk_send)

    @pl.when(is_source)
    def _():
        left(mc, q0_send)

    @pl.when(is_relay)
    def _():
        left(q0, q0_send)


def decompress(q_ref, merged, basis, upd_ref, err_ref, upd, err, sem):
    nd, rows, cb = merged.shape
    per = nd // GROUPS
    wide = per * cb
    left = basis[...]
    copies = []
    for i in range(GROUPS):
        for j in range(per):
            block = i * per + j
            q_t = jnp.concatenate([q_ref[0, block], q_ref[1, block]], axis=1)
            mean = jnp.dot(left, q_t, preferred_element_type=F32) * (1.0 / nd)
            cols = pl.ds(block * cb, cb)
            upd[:, cols] = mean.astype(BF16)
            err[:, cols] = (merged[block].astype(F32) - mean).astype(BF16)
        cols = pl.ds(i * wide, wide)
        for j, (src, dst) in enumerate(((upd, upd_ref), (err, err_ref.at[0]))):
            copy = pltpu.make_async_copy(src.at[:, cols], dst.at[:, cols], sem.at[j, i])
            copy.start()
            copies.append(copy)
    for copy in copies:
        copy.wait()


def on_device(gradient, error, warm_start):
    nd = NX * NZ
    _, rows, width = gradient.shape
    cb = width // nd
    dma = pltpu.SemaphoreType.DMA
    hbm = pl.BlockSpec(memory_space=pltpu.HBM)
    vmem = pl.BlockSpec(memory_space=pltpu.VMEM)
    small = (HALF, 2 * RANK)
    q, merged, basis = pl.pallas_call(
        kernel,
        out_shape=(
            pltpu.VMEM((2, nd, RANK, cb // 2), BF16),
            pltpu.VMEM((nd, rows, cb), BF16),
            pltpu.VMEM((rows, RANK), BF16),
        ),
        in_specs=[hbm, hbm, hbm],
        out_specs=(vmem, vmem, vmem),
        scratch_shapes=[
            pltpu.VMEM((rows, width), BF16),
            pltpu.VMEM((rows, width), BF16),
            pltpu.VMEM((NZ // 2, 2, 3 * rows - TAIL, cb), BF16),
            pltpu.VMEM((NZ - 1, rows, cb), BF16),
            pltpu.VMEM((NZ, rows, cb), BF16),
            pltpu.VMEM((NZ - 1, TAIL, cb), BF16),
            pltpu.VMEM((TAIL, cb), BF16),
            pltpu.VMEM((TAIL, cb), BF16),
            pltpu.VMEM((NY, rows, cb), BF16),
            pltpu.VMEM((RANK, cb), BF16),
            pltpu.VMEM((2, NX) + small, F32),
            pltpu.VMEM((2, NZ) + small, F32),
            pltpu.VMEM((2, NY) + small, F32),
            pltpu.VMEM((2, 2) + small, F32),
            pltpu.VMEM((2, 2, RANK, cb), F32),
            pltpu.VMEM((2, 8, 128), F32),
            dma((2,)), dma, dma, dma, dma, dma((NZ,)), dma, dma, dma, dma, dma, dma,
            dma, dma, dma, dma((2,)), dma, dma((2,)), dma, dma((2,)), dma, dma((2,)), dma, dma((2,)), dma, dma,
            dma, dma((NZ - 1,)), dma, dma((NZ,)), dma, dma, dma, dma, dma, dma, dma,
        ],
        compiler_params=pltpu.CompilerParams(collective_id=0, has_side_effects=True, vmem_limit_bytes=32 << 20),
        cost_estimate=pl.CostEstimate(flops=4 * rows * width * RANK, bytes_accessed=8 * rows * width, transcendentals=0),
    )(*(pltpu.with_memory_space_constraint(v, pltpu.HBM) for v in (gradient, error, warm_start.T)))
    q, merged, basis = (pltpu.with_memory_space_constraint(v, pltpu.VMEM) for v in (q, merged, basis))
    return pl.pallas_call(
        decompress,
        out_shape=(jax.ShapeDtypeStruct((rows, width), BF16), jax.ShapeDtypeStruct((1, rows, width), BF16)),
        in_specs=[vmem, vmem, vmem],
        out_specs=(hbm, hbm),
        scratch_shapes=[pltpu.VMEM((rows, width), BF16), pltpu.VMEM((rows, width), BF16), dma((2, GROUPS))],
        compiler_params=pltpu.CompilerParams(vmem_limit_bytes=16 << 20),
        cost_estimate=pl.CostEstimate(flops=2 * rows * width * RANK, bytes_accessed=8 * rows * width, transcendentals=0),
    )(q, merged, basis)


def solution(mesh):
    return jax.shard_map(
        on_device,
        mesh=mesh,
        in_specs=(P("dp", "fsdp", None), P("dp", "fsdp", None), P("fsdp", None)),
        out_specs=(P("fsdp", None), P("dp", "fsdp", None)),
        check_vma=False,
    )
```

```python
import functools

import jax
import jax.numpy as jnp
from jax import lax
from jax.experimental import pallas as pl
from jax.experimental.pallas import tpu as pltpu
from jax.sharding import PartitionSpec as P

MESH = pl.DeviceIdType.MESH
F32, BF16 = jnp.float32, jnp.bfloat16
NX, NY, NZ = 4, 8, 8
RANK = 64
HALF = RANK // 2
TAIL = 48
GROUPS = 4


def split(a):
    high = a.astype(BF16)
    rest = a - high.astype(F32)
    middle = rest.astype(BF16)
    return jnp.concatenate([high, middle, (rest - middle.astype(F32)).astype(BF16)], axis=0)


def exact(a, b, contract=((1,), (0,))):
    terms = lax.dot_general(a, b, (contract, ((), ())), preferred_element_type=F32)
    return terms[:RANK] + (terms[RANK : 2 * RANK] + terms[2 * RANK :])


def dot(a, b):
    return jnp.dot(a, b, precision=lax.Precision.HIGHEST, preferred_element_type=F32)


def by_distance(n):
    return sorted(range(1, n), key=lambda o: (-min(o, n - o), o))


def pack(a):
    return jnp.concatenate([a[:HALF], a[HALF:]], axis=1)


def unpack(a):
    return jnp.concatenate([a[:, :RANK], a[:, RANK:]], axis=0)


def inverse_factor(packed):
    lane = lax.broadcasted_iota(jnp.int32, (8, 2 * RANK), 1)
    sub = lax.broadcasted_iota(jnp.int32, (8, 2 * RANK), 0)
    rolled = pltpu.roll(packed, RANK, 1)
    full, n = (8, 2 * RANK), RANK // 8
    a = []
    for b in range(n):
        source = packed if b < n // 2 else rolled
        r = (8 * b) % HALF
        a.append(jnp.where(lane < RANK, source[r : r + 8], (lane - RANK == sub + 8 * b).astype(F32)))
    for b in range(n):
        row = [jnp.broadcast_to(a[b][j : j + 1, :], full) for j in range(8)]
        diag = {(i, j): jnp.broadcast_to(row[i][:, 8 * b + j : 8 * b + j + 1], full) for i in range(8) for j in range(i, 8)}
        column = {(j, v): jnp.broadcast_to(a[v][:, 8 * b + j : 8 * b + j + 1], full) for j in range(8) for v in range(b + 1, n)}
        scaled = []
        for j in range(8):
            inverse = 1.0 / diag[j, j]
            for i in range(j + 1, 8):
                factor = diag[j, i] * inverse
                for c in range(i, 8):
                    diag[i, c] = diag[i, c] - factor * diag[j, c]
                row[i] = row[i] - factor * row[j]
                for v in range(b + 1, n):
                    column[i, v] = column[i, v] - factor * column[j, v]
            scaled.append(row[j] * inverse)
        for v in range(b + 1, n):
            for j in range(8):
                a[v] = a[v] - column[j, v] * scaled[j]
        for j in range(1, 8):
            a[b] = jnp.where(sub == j, row[j], a[b])
    out = []
    for b in range(n):
        pivot = jnp.sum(jnp.where(lane == sub + 8 * b, a[b], 0.0), axis=1, keepdims=True)
        out.append(a[b] * lax.rsqrt(pivot))
    return jnp.concatenate(out, axis=0)[:, RANK:]


def kernel(
    g_ref, e_ref, w_ref, qland, merged, basis,
    gv, ev, xland, zsend, zland, tland, tsum, tx, mc, q0, px, pz, pf, gx, ux, nx,
    in_sem, w_sem, q0_send, q0_recv, x_send, x_recv, z_send, z_recv, t_send, t_recv, tx_send, tx_recv,
    my_send, my_recv, px_send, px_recv, pz_send, pz_recv, py_send, py_recv, gx_send, gx_recv, ux_send, ux_recv,
    nx_send, nx_recv,
    qz_send, qz_recv, qx_send, qx_recv, qu_send, qu_recv, qv_send, qv_recv, qw_recv, qk_send, qk_recv,
):
    nd, rows, cb = merged.shape
    body = rows - TAIL
    half = cb // 2
    d, f = lax.axis_index("dp"), lax.axis_index("fsdp")
    x, z, y, k = d // NZ, d % NZ, f // 2, f % 2

    def at_x(o):
        return {"dp": ((x + o) % NX) * NZ + z, "fsdp": f}

    def at_z(o):
        return {"dp": x * NZ + (z + o) % NZ, "fsdp": f}

    def at_y(o):
        return {"dp": d, "fsdp": ((y + o) % NY) * 2 + k}

    partner = {"dp": d, "fsdp": f + 1 - 2 * k}

    def remote(src, dst, ssem, rsem, to):
        return pltpu.make_async_remote_copy(
            src_ref=src, dst_ref=dst, send_sem=ssem, recv_sem=rsem, device_id=to, device_id_type=MESH
        )

    def send(src, dst, ssem, rsem, to):
        remote(src, dst, ssem, rsem, to).start()

    def arrived(as_much, sem):
        remote(as_much, as_much, sem, sem, partner).wait_recv()

    def left(as_much, sem):
        remote(as_much, as_much, sem, sem, partner).wait_send()

    loads = [pltpu.make_async_copy(g_ref.at[0], gv, in_sem.at[0]), pltpu.make_async_copy(e_ref.at[0], ev, in_sem.at[1])]
    for copy in loads:
        copy.start()

    barrier = pltpu.get_barrier_semaphore()
    greeted = [at_z(o) for o in by_distance(NZ)] + [at_y(o) for o in by_distance(NY)] + [at_x(o) for o in by_distance(NX)]
    greeted.append(partner)
    for to in greeted:
        pl.semaphore_signal(barrier, inc=1, device_id=to, device_id_type=MESH)

    per = w_ref.shape[1] // cb
    source = d // per
    w_copy = pltpu.make_async_copy(w_ref.at[:, pl.ds(pl.multiple_of((d % per) * cb, cb), cb)], q0, w_sem)
    is_source = f == source
    is_relay = (k == source % 2) & (y != source // 2)

    @pl.when(is_source)
    def _():
        w_copy.start()

    for copy in loads:
        copy.wait()

    zorder = by_distance(NZ) + [0]
    for i, o in enumerate(zorder):
        w = (z + o) % NZ
        for t in range(NX):
            block = t * NZ + w
            cols = pl.ds(pl.multiple_of(block * cb, cb), cb)
            merged[block] = (gv[:, cols].astype(F32) + ev[:, cols].astype(F32)).astype(BF16)
    pl.semaphore_wait(barrier, len(greeted))

    def mine(i, xo):
        return ((x + xo) % NX) * NZ + (z + zorder[i]) % NZ

    opposite = NX // 2
    pairs = [2, 1, 3, 0]

    def first_of(i):
        return 2 * ((z // 2 + pairs[i]) % (NZ // 2))

    def two(i, xo):
        return pl.ds(((x + xo) % NX) * NZ + first_of(i), 2)

    for i in range(NZ // 2):
        to = at_x(opposite)
        send(merged.at[two(i, opposite), pl.ds(0, body)], xland.at[i, :, pl.ds(2 * rows, body)], x_send, x_recv.at[i], to)
        for j in range(2):
            xo = 1 - 2 * j
            send(merged.at[two(i, xo)], xland.at[i, :, pl.ds(j * rows, rows)], x_send, x_recv.at[i], at_x(xo))
        for h in (2 * i, 2 * i + 1):
            if h < NZ - 1:
                send(merged.at[mine(h, opposite), pl.ds(body, TAIL)], tland.at[h], t_send, t_recv, at_z(zorder[h]))

    @pl.when(is_source)
    def _():
        w_copy.wait()
        send(q0, q0, q0_send, q0_recv, partner)
        for o in by_distance(NY):
            send(q0, q0, q0_send, q0_recv, at_y(o))

    def finish_tails():
        arrived(tland, t_recv)
        total = merged[mine(NZ - 1, opposite)][body:].astype(F32)
        for i in range(NZ - 1):
            total = total + tland[i].astype(F32)
        tsum[...] = total.astype(BF16)
        send(tsum, tx, tx_send, tx_recv, at_x(opposite))

    def block_sum(i, b):
        landed = xland[i, b].astype(F32)
        total = merged[x * NZ + first_of(i) + b].astype(F32) + (landed[:rows] + landed[rows : 2 * rows])
        return jnp.concatenate([total[:body] + landed[2 * rows :], total[body:]], axis=0)

    for i in range(NZ // 2):
        if i == NZ // 2 - 1:
            @pl.when(is_relay)
            def _():
                arrived(q0, q0_recv)
                send(q0, q0, q0_send, q0_recv, partner)

        arrived(xland.at[i], x_recv.at[i])
        if i == NZ // 2 - 1:
            finish_tails()
        for b in range(2) if i < NZ // 2 - 1 else (1 - z % 2,):
            at = 2 * i if i == NZ // 2 - 1 else 2 * i + b
            zsend[at] = block_sum(i, b).astype(BF16)
            to = {"dp": x * NZ + first_of(i) + b, "fsdp": f}
            send(zsend.at[at], zland.at[z], z_send, z_recv, to)
    total = block_sum(NZ // 2 - 1, z % 2)
    arrived(zland.at[pl.ds(0, NZ - 1)], z_recv)
    for o in range(1, NZ):
        total = total + zland[(z + o) % NZ].astype(F32)
    arrived(tx, tx_recv)
    m = jnp.concatenate([total[:body], total[body:] + tx[...].astype(F32)], axis=0).astype(BF16)

    @pl.when(~(is_source | is_relay))
    def _():
        arrived(q0, q0_recv)

    mc[y] = m
    for o in by_distance(NY):
        send(mc.at[y], mc.at[y], my_send, my_recv, at_y(o))

    def sum_dp(value, use, beside=None):
        px[use, x] = pack(value)
        for o in by_distance(NX):
            send(px.at[use, x], px.at[use, x], px_send, px_recv.at[use], at_x(o))
        arrived(px.at[use, pl.ds(0, NX - 1)], px_recv.at[use])
        total = (px[use, 0] + px[use, 1]) + (px[use, 2] + px[use, 3])
        pz[use, z] = total
        for o in by_distance(NZ):
            send(pz.at[use, z], pz.at[use, z], pz_send, pz_recv.at[use], at_z(o))
        extra = beside() if beside is not None else None
        arrived(pz.at[use, pl.ds(0, NZ - 1)], pz_recv.at[use])
        total = pz[use, 0]
        for i in range(1, NZ):
            total = total + pz[use, i]
        return total, extra

    lane = lax.broadcasted_iota(jnp.int32, (HALF, 2 * RANK), 1)

    def over_rows(packed, use, factor=None):
        pf[use, y] = packed
        for o in by_distance(NY):
            send(pf.at[use, y], pf.at[use, y], py_send, py_recv.at[use], at_y(o))
        if use == 0:
            arrived(mc.at[pl.ds(0, NY - 1)], my_recv)
        arrived(pf.at[use, pl.ds(0, NY - 1)], py_recv.at[use])
        if use == 0:
            norm = pf[use, 0] * pf[use, 0]
            for i in range(1, NY):
                norm = norm + pf[use, i] * pf[use, i]
            nx[k] = (norm[:8] + norm[8:16]) + (norm[16:24] + norm[24:])
            send(nx.at[k], nx.at[k], nx_send, nx_recv, partner)
        terms = []
        for i in range(0, NY, 4):
            parts = []
            for j in range(i, i + 4, 2):
                one, two = pf[use, j], pf[use, j + 1]
                upper = jnp.where(lane < RANK, one, pltpu.roll(two, RANK, 1))
                lower = jnp.where(lane < RANK, pltpu.roll(one, RANK, 1), two)
                parts.append(jnp.concatenate([upper, lower], axis=0))
            p = jnp.concatenate(parts, axis=1)
            terms.append(split(p if factor is None else dot(factor, p)))

        def start_gram():
            gram = sum(exact(p, p, ((1,), (1,))) for p in terms)
            gx[use, k] = pack(gram[:, :RANK] + (gram[:, RANK : 2 * RANK] + gram[:, 2 * RANK :]))
            send(gx.at[use, k], gx.at[use, k], gx_send, gx_recv.at[use], partner)

        def start_right():
            ux[use, k] = sum(exact(p, mc[4 * i : 4 * i + 4].reshape(4 * rows, cb)) for i, p in enumerate(terms))
            send(ux.at[use, k], ux.at[use, k], ux_send, ux_recv.at[use], partner)

        for start in (start_right, start_gram) if use == 0 else (start_gram, start_right):
            start()

        def gram():
            arrived(gx.at[use, 1 - k], gx_recv.at[use])
            return gx[use, 0] + gx[use, 1]

        def right():
            arrived(ux.at[use, 1 - k], ux_recv.at[use])
            return ux[use, 0] + ux[use, 1]

        return gram, right

    p, _ = sum_dp(
        lax.dot_general(q0[...], m, (((1,), (1,)), ((), ())), preferred_element_type=F32), 0
    )
    gram, right = over_rows(p, 0)
    arrived(nx.at[1 - k], nx_recv)
    scale = lax.rsqrt(jnp.sum(jnp.sum(nx[0] + nx[1], axis=0, keepdims=True), axis=1, keepdims=True))
    u_t = right()

    p, inverse = sum_dp(
        exact(split(u_t * scale), mc[y], ((1,), (1,))), 1, lambda: inverse_factor(gram() * scale * scale)
    )
    gram, right = over_rows(p, 1, inverse)
    p_t = dot(inverse, unpack(p))
    inverse = inverse_factor(gram())
    q_t = dot(inverse, right())
    qland[k, d] = jnp.where(k == 0, q_t[:, :half], q_t[:, half:]).astype(BF16)

    for o in by_distance(NZ)[::-1]:
        send(qland.at[k, d], qland.at[k, d], qz_send, qz_recv.at[o - 1], at_z(o))
    first, last = pl.ds(0, RANK // 4), pl.ds(RANK // 4, 3 * RANK // 4)

    def to_x(block, at):
        send(qland.at[k, block, first], qland.at[k, block, first], qu_send, qu_recv, at_x(opposite))
        for j in range(2):
            send(qland.at[k, block], qland.at[k, block], qx_send, qx_recv.at[at], at_x(1 - 2 * j))

    send(qland.at[k, d, last], qland.at[k, d, last], qv_send, qv_recv, at_x(opposite))
    to_x(d, 0)
    basis[...] = dot(inverse, p_t).T.astype(BF16)
    facing = ((x + opposite) % NX) * NZ
    near = by_distance(NZ)[::-1]
    for i, o in enumerate(near):
        block = x * NZ + (z - o) % NZ
        arrived(qland.at[k, block], qz_recv.at[o - 1])
        to_x(block, o)
        if i == 1:
            arrived(qland.at[k, facing + z, last], qv_recv)
            for zo in by_distance(NZ):
                send(qland.at[k, facing + z, last], qland.at[k, facing + z, last], qv_send, qw_recv, at_z(zo))
    column = qland.at[k, pl.ds(x * NZ, NZ)]
    send(column, column, qk_send, qk_recv, partner)
    for o in [0] + near:
        arrived(qland.at[k, pl.ds(0, 2)], qx_recv.at[o])
        for j in range(2):
            block = ((x + 1 - 2 * j) % NX) * NZ + (z - o) % NZ
            send(qland.at[k, block], qland.at[k, block], qk_send, qk_recv, partner)
    arrived(qland.at[k, pl.ds(0, NZ - 1), last], qw_recv)
    arrived(qland.at[k, pl.ds(0, NZ), first], qu_recv)
    send(qland.at[k, pl.ds(facing, NZ)], qland.at[k, pl.ds(facing, NZ)], qk_send, qk_recv, partner)
    arrived(qland.at[1 - k], qk_recv)

    left(xland, x_send)
    left(tland, t_send)
    left(tx, tx_send)
    left(zsend, z_send)
    left(mc.at[pl.ds(0, NY - 1)], my_send)
    left(px.at[:, pl.ds(0, NX - 1)], px_send)
    left(pz.at[:, pl.ds(0, NZ - 1)], pz_send)
    left(pf.at[:, pl.ds(0, NY - 1)], py_send)
    left(gx.at[:, k], gx_send)
    left(ux.at[:, k], ux_send)
    left(nx.at[k], nx_send)
    left(qland.at[k, pl.ds(0, NZ - 1)], qz_send)
    left(qland.at[k, pl.ds(0, 2 * NZ)], qx_send)
    left(qland.at[k, pl.ds(0, NZ), first], qu_send)
    left(qland.at[k, pl.ds(0, NZ), last], qv_send)
    left(qland.at[k], qk_send)

    @pl.when(is_source)
    def _():
        left(mc, q0_send)

    @pl.when(is_relay)
    def _():
        left(q0, q0_send)


def decompress(q_ref, merged, basis, upd_ref, err_ref, upd, err, sem):
    nd, rows, cb = merged.shape
    per = nd // GROUPS
    wide = per * cb
    left = basis[...]
    copies = []
    for i in range(GROUPS):
        for j in range(per):
            block = i * per + j
            q_t = jnp.concatenate([q_ref[0, block], q_ref[1, block]], axis=1)
            mean = jnp.dot(left, q_t, preferred_element_type=F32) * (1.0 / nd)
            cols = pl.ds(block * cb, cb)
            upd[:, cols] = mean.astype(BF16)
            err[:, cols] = (merged[block].astype(F32) - mean).astype(BF16)
        cols = pl.ds(i * wide, wide)
        for j, (src, dst) in enumerate(((upd, upd_ref), (err, err_ref.at[0]))):
            copy = pltpu.make_async_copy(src.at[:, cols], dst.at[:, cols], sem.at[j, i])
            copy.start()
            copies.append(copy)
    for copy in copies:
        copy.wait()


def on_device(gradient, error, warm_start):
    nd = NX * NZ
    _, rows, width = gradient.shape
    cb = width // nd
    dma = pltpu.SemaphoreType.DMA
    hbm = pl.BlockSpec(memory_space=pltpu.HBM)
    vmem = pl.BlockSpec(memory_space=pltpu.VMEM)
    small = (HALF, 2 * RANK)
    q, merged, basis = pl.pallas_call(
        kernel,
        out_shape=(
            pltpu.VMEM((2, nd, RANK, cb // 2), BF16),
            pltpu.VMEM((nd, rows, cb), BF16),
            pltpu.VMEM((rows, RANK), BF16),
        ),
        in_specs=[hbm, hbm, hbm],
        out_specs=(vmem, vmem, vmem),
        scratch_shapes=[
            pltpu.VMEM((rows, width), BF16),
            pltpu.VMEM((rows, width), BF16),
            pltpu.VMEM((NZ // 2, 2, 3 * rows - TAIL, cb), BF16),
            pltpu.VMEM((NZ - 1, rows, cb), BF16),
            pltpu.VMEM((NZ, rows, cb), BF16),
            pltpu.VMEM((NZ - 1, TAIL, cb), BF16),
            pltpu.VMEM((TAIL, cb), BF16),
            pltpu.VMEM((TAIL, cb), BF16),
            pltpu.VMEM((NY, rows, cb), BF16),
            pltpu.VMEM((RANK, cb), BF16),
            pltpu.VMEM((2, NX) + small, F32),
            pltpu.VMEM((2, NZ) + small, F32),
            pltpu.VMEM((2, NY) + small, F32),
            pltpu.VMEM((2, 2) + small, F32),
            pltpu.VMEM((2, 2, RANK, cb), F32),
            pltpu.VMEM((2, 8, 128), F32),
            dma((2,)), dma, dma, dma, dma, dma((NZ,)), dma, dma, dma, dma, dma, dma,
            dma, dma, dma, dma((2,)), dma, dma((2,)), dma, dma((2,)), dma, dma((2,)), dma, dma((2,)), dma, dma,
            dma, dma((NZ - 1,)), dma, dma((NZ,)), dma, dma, dma, dma, dma, dma, dma,
        ],
        compiler_params=pltpu.CompilerParams(collective_id=0, has_side_effects=True, vmem_limit_bytes=32 << 20),
        cost_estimate=pl.CostEstimate(flops=4 * rows * width * RANK, bytes_accessed=8 * rows * width, transcendentals=0),
    )(*(pltpu.with_memory_space_constraint(v, pltpu.HBM) for v in (gradient, error, warm_start.T)))
    q, merged, basis = (pltpu.with_memory_space_constraint(v, pltpu.VMEM) for v in (q, merged, basis))
    return pl.pallas_call(
        decompress,
        out_shape=(jax.ShapeDtypeStruct((rows, width), BF16), jax.ShapeDtypeStruct((1, rows, width), BF16)),
        in_specs=[vmem, vmem, vmem],
        out_specs=(hbm, hbm),
        scratch_shapes=[pltpu.VMEM((rows, width), BF16), pltpu.VMEM((rows, width), BF16), dma((2, GROUPS))],
        compiler_params=pltpu.CompilerParams(vmem_limit_bytes=16 << 20),
        cost_estimate=pl.CostEstimate(flops=2 * rows * width * RANK, bytes_accessed=8 * rows * width, transcendentals=0),
    )(q, merged, basis)


def solution(mesh):
    return jax.shard_map(
        on_device,
        mesh=mesh,
        in_specs=(P("dp", "fsdp", None), P("dp", "fsdp", None), P("fsdp", None)),
        out_specs=(P("fsdp", None), P("dp", "fsdp", None)),
        check_vma=False,
    )
```
